32 devices in a mesh: grp: 2 (over y), pencil: 4 (over z), depth: 2 (over x), mem: 2 (over core).
Axes of the slice: x: 2, y: 2, z: 4, core: 2. Of those that a mesh axis runs over, the one named last changes fastest.
Arguments:
- density: float32 [4, 2, 2048, 2048], P(('grp', 'mem'), 'depth', 'pencil'), parts along dimension 0, may hold values from -6 to 6
- background: float32 [8, 2], P(None, 'depth'), may hold values from -2 to 2
- member_ids: int32 [4], P(('grp', 'mem')), parts along dimension 0, may hold values from 0 to 7
- layer_kernel: int32 [2], P('depth'), may hold values from 0 to 3, as said below
- kernel_spectra: bfloat16 [4, 2, 2048, 2048], P('depth', None, None, 'pencil'), may hold values from -4 to 4
Outputs:
- gravity: float32 [4, 2048, 2048], P(('grp', 'mem'), ('pencil', 'depth')), parts along dimension 0
The draws below stay inside these ranges and needn't reach their ends.
There are 2 independent parts, one for each index of `grp`. The reference program is written for one: setup_inputs(seed, part) draws one part's arguments, and reference() takes and returns one part's arrays. A program takes and returns all parts, laid end to end along the dimension named above; an argument that names none is the same for every part. Nothing has to cross between parts.
Inputs may be any that keep to these rules, and one draw needn't show every extreme that they name: Layer l takes one of the 2 kernels of its depth band: layer_kernel[l] // 2 equals l.
All inputs are finite; a program needn't handle non-finite values.
Results may differ from the reference program's by a relative error of at most 0.0003.
Values sent between devices are 32-bit elements; how exact they have to be, the bound alone decides.
A program may use at most 128 MiB of HBM per device.

```python
import jax
import jax.numpy as jnp
from jax import lax

NX = 2048
NY = 2048
LAY_DEV = 1
K_DEV = 2
PROFILES = 8
LAYERS = 2
NK = 4
MEMBERS = 2


def draw_layer_kernel(key, part):
    key_offset = jax.random.fold_in(key, 17)
    positions = jnp.arange(LAYERS, dtype=jnp.int32)
    offsets = jax.random.randint(key_offset, (LAYERS,), 0, K_DEV).astype(jnp.int32)
    offsets = jnp.where(positions == 0, 0, offsets)
    offsets = jnp.where(positions == LAYERS - 1, K_DEV - 1, offsets)
    return (positions // LAY_DEV * K_DEV + offsets).astype(jnp.int32)


def levels(stream_key, extent, pieces, low, high):
    factor_of = 1.0
    for dim, parts in pieces:
        draws = jax.random.uniform(jax.random.fold_in(jax.random.fold_in(stream_key, 6), dim), (parts,), jnp.float32, low / len(pieces), high / len(pieces))
        factor_of = factor_of * jnp.repeat(jnp.exp(draws), extent[dim] // parts).reshape((-1,) + (1,) * (len(extent) - 1 - dim))
    return factor_of


def scatter_about(own_key, shape, scale, most, split=(), held_as=jnp.bfloat16):
    entries = scale * jax.random.normal(own_key, shape, jnp.float32)
    if split:
        entries = entries * levels(own_key, shape, split, -0.22, 0.18)
    return jnp.clip(entries, -most, most).astype(held_as)


def setup_inputs(seed: int = 0, part: int = 0) -> dict:
    splits = jax.random.split(jax.random.key(seed), 6)
    part_keys = jax.random.split(jax.random.fold_in(splits[5], part), 6)
    return {
        "density": scatter_about(part_keys[0], (MEMBERS, LAYERS, NX, NY), 1.0, 6.0, ((0, 2), (1, 2), (2, 4)), jnp.float32),
        "background": jnp.clip(jax.random.uniform(splits[1], (PROFILES, LAYERS), jnp.float32, -2.0, 2.0) * levels(splits[1], (PROFILES, LAYERS), ((1, 2),), -0.4, 0.0), -2.0, 2.0),
        "member_ids": jax.random.randint(part_keys[2], (MEMBERS,), 0, PROFILES).astype(jnp.int32),
        "layer_kernel": draw_layer_kernel(jax.random.fold_in(splits[5], 71), part),
        "kernel_spectra": scatter_about(splits[4], (NK, 2, NX, NY), LAYERS ** -0.5, 4.0, ((0, 2), (3, 4))),
    }


def storage_order(length):
    frequency = jnp.arange(length, dtype=jnp.int32)
    return (frequency % 16) * (length // 16) + frequency // 16


def reference(density, background, member_ids, layer_kernel, kernel_spectra):
    order_x = storage_order(NX)
    order_y = storage_order(NY)
    outputs = []
    for member in range(MEMBERS):
        offsets = background[member_ids[member]]
        total_real = jnp.zeros((NX, NY), jnp.float32)
        total_imag = jnp.zeros((NX, NY), jnp.float32)
        for layer_pos in range(LAYERS):
            contrast = density[member, layer_pos] - offsets[layer_pos]
            transformed = jnp.fft.fft2(contrast)
            trans_real = jnp.real(transformed)
            trans_imag = jnp.imag(transformed)
            stored = kernel_spectra[layer_kernel[layer_pos]].astype(jnp.float32)
            kern_real = stored[0][order_x][:, order_y]
            kern_imag = stored[1][order_x][:, order_y]
            total_real = total_real + trans_real * kern_real - trans_imag * kern_imag
            total_imag = total_imag + trans_real * kern_imag + trans_imag * kern_real
        gravity_field = jnp.fft.ifft2(lax.complex(total_real, total_imag))
        outputs.append(jnp.real(gravity_field))
    return jnp.stack(outputs)
```

```python
import functools
import math

import jax
import jax.numpy as jnp
import numpy as np
from jax import lax
from jax.experimental import pallas as pl
from jax.experimental.pallas import tpu as pltpu
from jax.sharding import PartitionSpec as P

RADIX = 16
INNER = 128
HALF = 64
LENGTH = RADIX * INNER
f32 = jnp.float32
bf16 = jnp.bfloat16


def halves(table):
    table = np.asarray(table, np.float32)
    high = table.astype(bf16)
    low = (table - high.astype(np.float32)).astype(bf16)
    return jnp.asarray(high), jnp.asarray(low)


def residue_rows(r):
    m = np.arange(INNER)[:, None]
    q = np.arange(HALF)[None, :]
    turn = np.exp(-2j * np.pi * (((RADIX * q + r) * m) % LENGTH) / LENGTH)
    re, im = turn.real.copy(), turn.imag.copy()
    if r == 0:
        im[:, 0] = (-1.0) ** m[:, 0]
    out = np.zeros((2 * INNER, 2 * HALF))
    if r == 0:
        out[:INNER, :HALF], out[:INNER, HALF:] = re, im
    elif r == 8:
        out[INNER:, :HALF], out[INNER:, HALF:] = re, im
    else:
        sign = 1.0 if r < 8 else -1.0
        out[:INNER, :HALF], out[:INNER, HALF:] = re, im
        out[INNER:, :HALF], out[INNER:, HALF:] = -sign * im, sign * re
    return out


def slot_of(r):
    return 0 if r in (0, 8) else min(r, RADIX - r)


def row_tables():
    tables = np.zeros((8, 512, 256))
    for t in range(8):
        for odd in range(2):
            block = residue_rows(2 * t + odd)
            rows = slice(256 * odd, 256 * odd + 256)
            tables[t, rows, HALF * odd : HALF * odd + HALF] = block[:, :HALF]
            tables[t, rows, 128 + HALF * odd : 128 + HALF * odd + HALF] = block[:, HALF:]
    return tables


def inverse_row_tables():
    tables = np.zeros((8, 512, 256))
    scale = 1.0 / (LENGTH * LENGTH)
    for s in range(8):
        for place, r in enumerate((s, 8 if s == 0 else RADIX - s)):
            block = residue_rows(r).T.copy() * scale
            weight = np.full((2 * HALF, 1), 2.0 if r in (0, 8) else 1.0)
            if r == 0:
                weight[0] = weight[HALF] = 1.0
            block *= weight
            odd = r % 2
            tables[s, 256 * place + HALF * odd : 256 * place + HALF * odd + HALF] += block[:HALF]
            tables[s, 256 * place + 128 + HALF * odd : 256 * place + 128 + HALF * odd + HALF] += block[HALF:]
    return tables


def column_tables():
    q = np.arange(INNER)[:, None]
    m = np.arange(INNER)[None, :]
    tables = np.zeros((RADIX, 256, 256))
    for r in range(RADIX):
        turn = np.exp(-2j * np.pi * (((RADIX * q + r) * m) % LENGTH) / LENGTH)
        tables[r] = np.block([[turn.real, -turn.imag], [turn.imag, turn.real]])
    return tables


def split_value(value):
    high = value.astype(bf16)
    return high, (value - high.astype(f32)).astype(bf16)


def dot(a, b):
    return jnp.dot(a, b, preferred_element_type=f32)


def rotate(value, count, length, sign):
    re, im = value
    count %= length
    if count == 0:
        return value
    if 4 * count == length:
        return (im, -re) if sign < 0 else (-im, re)
    c = math.cos(2 * math.pi * count / length)
    s = sign * math.sin(2 * math.pi * count / length)
    if 8 * count == length:
        return ((re + im) * c, (im - re) * c) if sign < 0 else ((re - im) * c, (im + re) * c)
    return (re * c - im * s, re * s + im * c)


def plus(a, b):
    return (a[0] + b[0], a[1] + b[1])


def minus(a, b):
    return (a[0] - b[0], a[1] - b[1])


def transform(values, sign):
    length = len(values)
    if length == 1:
        return values
    even, odd = transform(values[0::2], sign), transform(values[1::2], sign)
    turned = [rotate(odd[k], k, length, sign) for k in range(length // 2)]
    return [plus(even[k], turned[k]) for k in range(length // 2)] + [
        minus(even[k], turned[k]) for k in range(length // 2)
    ]


def real_transform(values):
    length = len(values)
    if length == 2:
        return [(values[0] + values[1], None), (values[0] - values[1], None)]
    even, odd = real_transform(values[0::2]), real_transform(values[1::2])
    out = [None] * (length // 2 + 1)
    out[0] = (even[0][0] + odd[0][0], None)
    out[length // 2] = (even[0][0] - odd[0][0], None)
    quarter = length // 4
    for k in range(1, quarter):
        turned = rotate(odd[k], k, length, -1)
        out[k] = plus(even[k], turned)
        low = minus(even[k], turned)
        out[length // 2 - k] = (low[0], -low[1])
    out[quarter] = (even[quarter][0], -odd[quarter][0])
    return out


def real_inverse(values):
    half = len(values) - 1
    length = 2 * half
    if length == 2:
        return [values[0][0] + values[1][0], values[0][0] - values[1][0]]
    even, odd = [], []
    for k in range(half // 2 + 1):
        if k == 0:
            even.append((values[0][0] + values[half][0], None))
            odd.append((values[0][0] - values[half][0], None))
        elif k == half // 2:
            even.append((2.0 * values[k][0], None))
            odd.append((-2.0 * values[k][1], None))
        else:
            other = values[half - k]
            even.append((values[k][0] + other[0], values[k][1] - other[1]))
            odd.append(rotate((values[k][0] - other[0], values[k][1] + other[1]), k, length, 1))
    first, second = real_inverse(even), real_inverse(odd)
    return [x for pair in zip(first, second) for x in pair]


def rows_kernel(pencils, width, offset_ref, in_ref, high_ref, low_ref, *rest):
    outs, pieces = rest[:-1], rest[-1]
    rows = in_ref.shape[0]
    per = RADIX // pencils
    offset = offset_ref[0]

    def step(b, carry):
        at = pl.ds(pl.multiple_of(b * 8, 8), 8)
        values = [in_ref[at, n * INNER : (n + 1) * INNER] - offset for n in range(RADIX)]
        got = real_transform(values)
        pieces[0, at, :INNER] = got[0][0]
        pieces[0, at, INNER:] = got[8][0]
        for s in range(1, 8):
            pieces[s, at, :INNER] = got[s][0]
            pieces[s, at, INNER:] = got[s][1]
        return carry

    lax.fori_loop(0, rows // 8, step, 0)
    for t in range(8):
        total = None
        for odd in range(2):
            high, low = split_value(pieces[slot_of(2 * t + odd)])
            table_high = high_ref[t, 256 * odd : 256 * odd + 256]
            table_low = low_ref[t, 256 * odd : 256 * odd + 256]
            part = dot(high, table_high) + dot(low, table_high) + dot(high, table_low)
            total = part if total is None else total + part
        if width == 2:
            pencil, place = divmod(2 * t, per)
            for c in range(2):
                outs[place // 2][pencil, c] = total[:, c * 128 : (c + 1) * 128]
        else:
            for odd in range(2):
                pencil, place = divmod(2 * t + odd, per)
                for c in range(2):
                    begin = c * 128 + odd * HALF
                    outs[place][pencil, c] = total[:, begin : begin + HALF]


def columns_kernel(special, mine_ref, in_ref, kern_ref, mirror_ref, swap_ref, fh_ref, fl_ref, ih_ref, il_ref,
                   out_ref, pieces, waves):
    part_rows = in_ref.shape[2]
    depths, pencils, _, out_rows, _ = out_ref.shape
    mine = mine_ref[0]

    def forward(b, carry):
        values = []
        for n in range(RADIX):
            source, begin = divmod(n * INNER, part_rows)
            at = pl.ds(pl.multiple_of(begin + b * 8, 8), 8)
            values.append((in_ref[source, 0, at, :], in_ref[source, 1, at, :]))
        at = pl.ds(pl.multiple_of(b * 8, 8), 8)
        also = pl.ds(pl.multiple_of(INNER + b * 8, 8), 8)
        for r, (re, im) in enumerate(transform(values, -1)):
            pieces[r, at, :] = re
            pieces[r, also, :] = im
        return carry

    lax.fori_loop(0, INNER // 8, forward, 0)

    def wave(r):
        high, low = split_value(pieces[r])
        return dot(fh_ref[r], high) + dot(fh_ref[r], low) + dot(fl_ref[r], high)

    def finish(r, got, extra):
        re, im = got[:INNER], got[INNER:]
        kr, ki = kern_ref[0, r], kern_ref[1, r]
        sr, si = re * kr - im * ki, re * ki + im * kr
        if extra is not None:
            sr, si = sr + extra[0], si + extra[1]
        spectrum = jnp.concatenate([sr, si], axis=0)
        high, low = split_value(spectrum)
        pieces[r] = dot(ih_ref[r], high) + dot(ih_ref[r], low) + dot(il_ref[r], high)

    if special:
        for r in range(RADIX):
            waves[r] = wave(r)
        for r in range(RADIX):
            other = (RADIX - r) % RADIX
            high, low = split_value(waves[other])
            swap = swap_ref[0 if r == 0 else 1]
            re = dot(swap, high[:INNER]) + dot(swap, low[:INNER])
            im = -(dot(swap, high[INNER:]) + dot(swap, low[INNER:]))
            kr, ki = mirror_ref[0, r], mirror_ref[1, r]
            finish(r, waves[r], (re * kr - im * ki, re * ki + im * kr))
    else:
        for r in range(RADIX):
            finish(r, wave(r), None)

    def backward(b, carry):
        at = pl.ds(pl.multiple_of(b * 8, 8), 8)
        also = pl.ds(pl.multiple_of(INNER + b * 8, 8), 8)
        values = [(pieces[r, at, :], pieces[r, also, :]) for r in range(RADIX)]
        for n, (re, im) in enumerate(transform(values, 1)):
            x = n * INNER + b * 8
            pencil = x // (out_rows * depths)
            depth = lax.rem(x // out_rows - mine + depths, depths)
            put = pl.ds(pl.multiple_of(lax.rem(x, out_rows), 8), 8)
            out_ref[depth, pencil, 0, put, :] = re
            out_ref[depth, pencil, 1, put, :] = im
        return carry

    lax.fori_loop(0, INNER // 8, backward, 0)


def fields_kernel(pencils, width, *refs):
    chunks = RADIX // pencils // width
    ins, (high_ref, low_ref, out_ref, pieces) = refs[:chunks], refs[chunks:]
    per = RADIX // pencils
    rows = out_ref.shape[1]

    def pair(t):
        if width == 2:
            pencil, place = divmod(2 * t, per)
            ref = ins[place // 2]
            return jnp.concatenate([ref[pencil, 0], ref[pencil, 1]], axis=1)
        found = []
        for c in range(2):
            for odd in range(2):
                pencil, place = divmod(2 * t + odd, per)
                found.append(ins[place][pencil, c])
        return jnp.concatenate(found, axis=1)

    for s in range(8):
        total = None
        for place, r in enumerate((s, 8 if s == 0 else RADIX - s)):
            high, low = split_value(pair(r // 2))
            table_high = high_ref[s, 256 * place : 256 * place + 256]
            table_low = low_ref[s, 256 * place : 256 * place + 256]
            part = dot(high, table_high) + dot(low, table_high) + dot(high, table_low)
            total = part if total is None else total + part
        pieces[s] = total

    def step(b, carry):
        at = pl.ds(pl.multiple_of(b * 8, 8), 8)
        values = [(pieces[0, at, :INNER], None)]
        for s in range(1, 8):
            values.append((pieces[s, at, :INNER], pieces[s, at, INNER:]))
        values.append((pieces[0, at, INNER:], None))
        for n, value in enumerate(real_inverse(values)):
            out_ref[0, at, n * INNER : (n + 1) * INNER] = value
        return carry

    lax.fori_loop(0, rows // 8, step, 0)


def params(**more):
    return pltpu.CompilerParams(vmem_limit_bytes=48 * 1024 * 1024, **more)


def body(density, background, member_ids, layer_kernel, kernel_spectra):
    pencils = lax.axis_size("pencil")
    depths = lax.axis_size("depth")
    sharers = lax.axis_size("grp") * lax.axis_size("mem")
    pencil = lax.axis_index("pencil")
    per = RADIX // pencils
    width = min(per, 2)
    chunks = per // width
    lanes = width * HALF
    part_rows = density.shape[2]
    out_rows = part_rows // depths
    vmem = pl.BlockSpec(memory_space=pltpu.VMEM)
    smem = pl.BlockSpec(memory_space=pltpu.SMEM)

    kern_count = kernel_spectra.shape[0]
    local = layer_kernel[0] - lax.axis_index("depth") * kern_count
    kernel = lax.dynamic_index_in_dim(kernel_spectra, local, 0, keepdims=False)
    kernel = kernel.reshape(2, RADIX, INNER, per, INNER)
    share = RADIX // sharers
    first = lax.axis_index(("grp", "mem")) * share
    taken = jnp.stack(
        [
            lax.dynamic_index_in_dim(kernel, lax.rem(RADIX - first - i, RADIX), 1, keepdims=False)
            for i in range(share)
        ],
        axis=0,
    )
    shape = (share, INNER, INNER)
    to = lax.broadcasted_iota(jnp.int32, shape, 1)
    is_zero = (lax.broadcasted_iota(jnp.int32, shape, 0) + first) == 0
    swap_x = (
        lax.broadcasted_iota(jnp.int32, shape, 2) == jnp.where(is_zero, (INNER - to) % INNER, INNER - 1 - to)
    ).astype(bf16)
    shape = (per, INNER, HALF)
    to = lax.broadcasted_iota(jnp.int32, shape, 2)
    is_zero = (lax.broadcasted_iota(jnp.int32, shape, 0) + pencil) == 0
    swap_y = (
        lax.broadcasted_iota(jnp.int32, shape, 1) == jnp.where(is_zero, (INNER - to) % INNER, INNER - 1 - to)
    ).astype(bf16)
    turned = jnp.einsum("icbjq,jqt->jibct", taken, swap_y, preferred_element_type=bf16)
    turned = turned.reshape(per, share, INNER, 2 * HALF)
    turned = jnp.einsum("iab,jibs->jias", swap_x, turned, preferred_element_type=f32)
    mirrored = lax.ppermute(turned[:1], "pencil", [(p, (pencils - p) % pencils) for p in range(pencils)])
    if per > 1:
        rest = lax.ppermute(
            turned[:0:-1], "pencil", [(p, pencils - 1 - p) for p in range(pencils)]
        )
        mirrored = jnp.concatenate([mirrored, rest], axis=0)
    mirrored = lax.all_gather(mirrored, ("grp", "mem"), axis=1, tiled=True)

    offset = lax.dynamic_index_in_dim(background[:, 0], member_ids[0], 0, keepdims=True)
    row_high, row_low = halves(row_tables())
    block = min(part_rows, 128)
    sent = pl.pallas_call(
        functools.partial(rows_kernel, pencils, width),
        grid=(part_rows // block,),
        in_specs=[
            smem,
            pl.BlockSpec((None, None, block, LENGTH), lambda i: (0, 0, i, 0)),
            pl.BlockSpec((8, 512, 256), lambda i: (0, 0, 0)),
            pl.BlockSpec((8, 512, 256), lambda i: (0, 0, 0)),
        ],
        out_specs=[pl.BlockSpec((pencils, 2, block, lanes), lambda i: (0, 0, i, 0))] * chunks,
        out_shape=[jax.ShapeDtypeStruct((pencils, 2, part_rows, lanes), f32)] * chunks,
        scratch_shapes=[pltpu.VMEM((8, block, 256), f32)],
        compiler_params=params(),
        cost_estimate=pl.CostEstimate(flops=6 * part_rows * 2 * LENGTH * 512, bytes_accessed=12 << 20, transcendentals=0),
    )(offset, density, row_high, row_low)
    arrived = [lax.all_to_all(part, "pencil", 0, 0, tiled=True) for part in sent]

    own = kernel[..., :HALF].astype(f32)
    sign = jnp.array([0.5, -0.5], f32)
    mirrored = mirrored.reshape(per, RADIX, INNER, 2, HALF).transpose(3, 1, 2, 0, 4)
    hermitian = 0.5 * own + sign.reshape(2, 1, 1, 1, 1) * mirrored
    edge = kernel[:, :, :, 0, HALF].astype(f32)
    flipped = jnp.concatenate([edge[:, :1], edge[:, :0:-1]], axis=1)[..., ::-1]
    flipped = jnp.concatenate([jnp.roll(flipped[:, :1], 1, axis=2), flipped[:, 1:]], axis=1)
    edge = 0.5 * edge + sign.reshape(2, 1, 1) * flipped
    zero = hermitian[..., 0, 0]
    both = jnp.where(pencil == 0, 0.5 * (zero + edge), zero)
    apart = jnp.where(pencil == 0, 0.5 * (zero - edge), 0.0)
    place = lax.broadcasted_iota(jnp.int32, (per, HALF), 0) + lax.broadcasted_iota(jnp.int32, (per, HALF), 1)
    hermitian = jnp.where(place == 0, both[..., None, None], hermitian)
    apart = jnp.where(lax.broadcasted_iota(jnp.int32, (lanes,), 0) == 0, apart[..., None], 0.0)

    column = column_tables()
    tables = halves(column) + halves(column.transpose(0, 2, 1))
    index = np.arange(INNER)
    swaps = np.zeros((2, INNER, INNER), np.float32)
    swaps[0, index, (INNER - index) % INNER] = 1.0
    swaps[1, index, INNER - 1 - index] = 1.0
    swaps = jnp.asarray(swaps.astype(bf16))
    two = depths == 2
    mine = lax.axis_index("depth") if two else jnp.int32(0)
    mine = mine.reshape(1)
    fields = []
    for k in range(chunks):
        factors = hermitian[..., k * width : (k + 1) * width, :].reshape(2, RADIX, INNER, lanes)
        special = k == 0
        out = pl.pallas_call(
            functools.partial(columns_kernel, special),
            in_specs=[smem] + [vmem] * 8,
            out_specs=vmem,
            out_shape=jax.ShapeDtypeStruct((depths, pencils, 2, out_rows, lanes), f32),
            scratch_shapes=[
                pltpu.VMEM((RADIX, 256, lanes), f32),
                pltpu.VMEM((RADIX if special else 1, 256, lanes), f32),
            ],
            compiler_params=params(),
            cost_estimate=pl.CostEstimate(flops=12 * RADIX * 256 * 256 * lanes, bytes_accessed=16 << 20, transcendentals=0),
        )(mine, arrived[k], factors, apart if special else apart[:, :1, :8], swaps, *tables)
        if two:
            out = out[0] + lax.ppermute(out[1], "depth", [(0, 1), (1, 0)])
        else:
            out = lax.psum_scatter(out, "depth", scatter_dimension=0, tiled=False)
        fields.append(lax.all_to_all(out, "pencil", 0, 0, tiled=True))

    back_high, back_low = halves(inverse_row_tables())
    return pl.pallas_call(
        functools.partial(fields_kernel, pencils, width),
        in_specs=[vmem] * (chunks + 2),
        out_specs=vmem,
        out_shape=jax.ShapeDtypeStruct((1, out_rows, LENGTH), f32),
        scratch_shapes=[pltpu.VMEM((8, out_rows, 256), f32)],
        compiler_params=params(),
        cost_estimate=pl.CostEstimate(flops=6 * out_rows * 2 * LENGTH * 512, bytes_accessed=8 << 20, transcendentals=0),
    )(*fields, back_high, back_low)


def solution(mesh):
    placed = (
        P(("grp", "mem"), "depth", "pencil", None),
        P(None, "depth"),
        P(("grp", "mem")),
        P("depth"),
        P("depth", None, None, "pencil"),
    )
    return jax.shard_map(
        body,
        mesh=mesh,
        in_specs=placed,
        out_specs=P(("grp", "mem"), ("pencil", "depth"), None),
        check_vma=False,
    )
```

```python
import functools
import math

import jax
import jax.numpy as jnp
import numpy as np
from jax import lax
from jax.experimental import pallas as pl
from jax.experimental.pallas import tpu as pltpu
from jax.sharding import PartitionSpec as P

RADIX = 16
INNER = 128
HALF = 64
LENGTH = RADIX * INNER
f32 = jnp.float32
bf16 = jnp.bfloat16


def halves(table):
    table = np.asarray(table, np.float32)
    high = table.astype(bf16)
    low = (table - high.astype(np.float32)).astype(bf16)
    return jnp.asarray(high), jnp.asarray(low)


def residue_rows(r):
    m = np.arange(INNER)[:, None]
    q = np.arange(HALF)[None, :]
    turn = np.exp(-2j * np.pi * (((RADIX * q + r) * m) % LENGTH) / LENGTH)
    re, im = turn.real.copy(), turn.imag.copy()
    if r == 0:
        im[:, 0] = (-1.0) ** m[:, 0]
    out = np.zeros((2 * INNER, 2 * HALF))
    if r == 0:
        out[:INNER, :HALF], out[:INNER, HALF:] = re, im
    elif r == 8:
        out[INNER:, :HALF], out[INNER:, HALF:] = re, im
    else:
        sign = 1.0 if r < 8 else -1.0
        out[:INNER, :HALF], out[:INNER, HALF:] = re, im
        out[INNER:, :HALF], out[INNER:, HALF:] = -sign * im, sign * re
    return out


def slot_of(r):
    return 0 if r in (0, 8) else min(r, RADIX - r)


def row_tables():
    tables = np.zeros((8, 512, 256))
    for t in range(8):
        for odd in range(2):
            block = residue_rows(2 * t + odd)
            rows = slice(256 * odd, 256 * odd + 256)
            tables[t, rows, HALF * odd : HALF * odd + HALF] = block[:, :HALF]
            tables[t, rows, 128 + HALF * odd : 128 + HALF * odd + HALF] = block[:, HALF:]
    return tables


def inverse_row_tables():
    tables = np.zeros((8, 512, 256))
    scale = 1.0 / (LENGTH * LENGTH)
    for s in range(8):
        for place, r in enumerate((s, 8 if s == 0 else RADIX - s)):
            block = residue_rows(r).T.copy() * scale
            weight = np.full((2 * HALF, 1), 2.0 if r in (0, 8) else 1.0)
            if r == 0:
                weight[0] = weight[HALF] = 1.0
            block *= weight
            odd = r % 2
            tables[s, 256 * place + HALF * odd : 256 * place + HALF * odd + HALF] += block[:HALF]
            tables[s, 256 * place + 128 + HALF * odd : 256 * place + 128 + HALF * odd + HALF] += block[HALF:]
    return tables


def column_tables():
    q = np.arange(INNER)[:, None]
    m = np.arange(INNER)[None, :]
    tables = np.zeros((RADIX, 256, 256))
    for r in range(RADIX):
        turn = np.exp(-2j * np.pi * (((RADIX * q + r) * m) % LENGTH) / LENGTH)
        tables[r] = np.block([[turn.real, -turn.imag], [turn.imag, turn.real]])
    return tables


def split_value(value):
    high = value.astype(bf16)
    return high, (value - high.astype(f32)).astype(bf16)


def dot(a, b):
    return jnp.dot(a, b, preferred_element_type=f32)


def rotate(value, count, length, sign):
    re, im = value
    count %= length
    if count == 0:
        return value
    if 4 * count == length:
        return (im, -re) if sign < 0 else (-im, re)
    c = math.cos(2 * math.pi * count / length)
    s = sign * math.sin(2 * math.pi * count / length)
    if 8 * count == length:
        return ((re + im) * c, (im - re) * c) if sign < 0 else ((re - im) * c, (im + re) * c)
    return (re * c - im * s, re * s + im * c)


def plus(a, b):
    return (a[0] + b[0], a[1] + b[1])


def minus(a, b):
    return (a[0] - b[0], a[1] - b[1])


def transform(values, sign):
    length = len(values)
    if length == 1:
        return values
    even, odd = transform(values[0::2], sign), transform(values[1::2], sign)
    turned = [rotate(odd[k], k, length, sign) for k in range(length // 2)]
    return [plus(even[k], turned[k]) for k in range(length // 2)] + [
        minus(even[k], turned[k]) for k in range(length // 2)
    ]


def real_transform(values):
    length = len(values)
    if length == 2:
        return [(values[0] + values[1], None), (values[0] - values[1], None)]
    even, odd = real_transform(values[0::2]), real_transform(values[1::2])
    out = [None] * (length // 2 + 1)
    out[0] = (even[0][0] + odd[0][0], None)
    out[length // 2] = (even[0][0] - odd[0][0], None)
    quarter = length // 4
    for k in range(1, quarter):
        turned = rotate(odd[k], k, length, -1)
        out[k] = plus(even[k], turned)
        low = minus(even[k], turned)
        out[length // 2 - k] = (low[0], -low[1])
    out[quarter] = (even[quarter][0], -odd[quarter][0])
    return out


def real_inverse(values):
    half = len(values) - 1
    length = 2 * half
    if length == 2:
        return [values[0][0] + values[1][0], values[0][0] - values[1][0]]
    even, odd = [], []
    for k in range(half // 2 + 1):
        if k == 0:
            even.append((values[0][0] + values[half][0], None))
            odd.append((values[0][0] - values[half][0], None))
        elif k == half // 2:
            even.append((2.0 * values[k][0], None))
            odd.append((-2.0 * values[k][1], None))
        else:
            other = values[half - k]
            even.append((values[k][0] + other[0], values[k][1] - other[1]))
            odd.append(rotate((values[k][0] - other[0], values[k][1] + other[1]), k, length, 1))
    first, second = real_inverse(even), real_inverse(odd)
    return [x for pair in zip(first, second) for x in pair]


def rows_kernel(pencils, width, offset_ref, in_ref, high_ref, low_ref, *rest):
    outs, pieces = rest[:-1], rest[-1]
    rows = in_ref.shape[0]
    per = RADIX // pencils
    offset = offset_ref[0]

    def step(b, carry):
        at = pl.ds(pl.multiple_of(b * 8, 8), 8)
        values = [in_ref[at, n * INNER : (n + 1) * INNER] - offset for n in range(RADIX)]
        got = real_transform(values)
        pieces[0, at, :INNER] = got[0][0]
        pieces[0, at, INNER:] = got[8][0]
        for s in range(1, 8):
            pieces[s, at, :INNER] = got[s][0]
            pieces[s, at, INNER:] = got[s][1]
        return carry

    lax.fori_loop(0, rows // 8, step, 0)
    for t in range(8):
        total = None
        for odd in range(2):
            high, low = split_value(pieces[slot_of(2 * t + odd)])
            table_high = high_ref[t, 256 * odd : 256 * odd + 256]
            table_low = low_ref[t, 256 * odd : 256 * odd + 256]
            part = dot(high, table_high) + dot(low, table_high) + dot(high, table_low)
            total = part if total is None else total + part
        if width == 2:
            pencil, place = divmod(2 * t, per)
            for c in range(2):
                outs[place // 2][pencil, c] = total[:, c * 128 : (c + 1) * 128]
        else:
            for odd in range(2):
                pencil, place = divmod(2 * t + odd, per)
                for c in range(2):
                    begin = c * 128 + odd * HALF
                    outs[place][pencil, c] = total[:, begin : begin + HALF]


def mirror_kernel(where_ref, in_ref, swap_ref, turn_ref, zero_ref, *rest_refs):
    per = in_ref.shape[2] // INNER
    swap = swap_ref[jnp.where(where_ref[1] + pl.program_id(0) == 0, 0, 1)]
    for j in range(per):
        turn = turn_ref[jnp.where(where_ref[2] == 0, 0, 1) if j == 0 else 1]
        turned = [dot(in_ref[c, :, j * INNER : (j + 1) * INNER], turn) for c in range(2)]
        value = dot(swap, jnp.concatenate(turned, axis=1).astype(bf16))
        if j == 0:
            zero_ref[0, 0] = value
        else:
            rest_refs[0][per - 1 - j, 0] = value


def columns_kernel(special, where_ref, in_ref, kern_ref, mirror_ref, edge_ref, swap_ref, pick_ref,
                   fh_ref, fl_ref, ih_ref, il_ref, out_ref, pieces, waves):
    part_rows = in_ref.shape[2]
    depths, pencils, _, out_rows, lanes = out_ref.shape
    share = mirror_ref.shape[1]
    steps = RADIX // share
    mine = where_ref[0]
    now = pl.program_id(0)

    def forward(b, carry):
        values = []
        for n in range(RADIX):
            source, begin = divmod(n * INNER, part_rows)
            at = pl.ds(pl.multiple_of(begin + b * 8, 8), 8)
            values.append((in_ref[source, 0, at, :], in_ref[source, 1, at, :]))
        at = pl.ds(pl.multiple_of(b * 8, 8), 8)
        also = pl.ds(pl.multiple_of(INNER + b * 8, 8), 8)
        for r, (re, im) in enumerate(transform(values, -1)):
            pieces[r, at, :] = re
            pieces[r, also, :] = im
        return carry

    @pl.when(now == 0)
    def _():
        lax.fori_loop(0, INNER // 8, forward, 0)

    def wave(r, u):
        high, low = split_value(pieces[r])
        return dot(fh_ref[u], high) + dot(fh_ref[u], low) + dot(fl_ref[u], high)

    def finish(r, u, got):
        re, im = got[:INNER], got[INNER:]
        tiles = [mirror_ref[j, u] for j in range(mirror_ref.shape[0])]
        rows = slice(u * INNER, (u + 1) * INNER)
        parts = []
        for c in range(2):
            other = [tile[:, c * HALF : (c + 1) * HALF] for tile in tiles]
            other = jnp.concatenate(other, axis=1) if len(other) > 1 else other[0]
            own = dot(kern_ref[c, rows, :], pick_ref[...])
            parts.append(own + 0.5 * other if c == 0 else own - 0.5 * other)
        kr, ki = parts
        if special:
            other = lax.rem(RADIX - r, RADIX)
            high, low = split_value(waves[other])
            swap = swap_ref[jnp.where(r == 0, 0, 1)]
            ore = dot(swap, high[:INNER]) + dot(swap, low[:INNER])
            oim = -(dot(swap, high[INNER:]) + dot(swap, low[INNER:]))
            mask = (lax.broadcasted_iota(jnp.int32, (INNER, lanes), 1) == 0) & (where_ref[2] == 0)
            hr = jnp.where(mask, 0.5 * (kr - edge_ref[0, u]), 0.0)
            hi = jnp.where(mask, 0.5 * (ki - edge_ref[1, u]), 0.0)
            kr, ki = kr - hr, ki - hi
            sr = re * kr - im * ki + (ore * hr - oim * hi)
            si = re * ki + im * kr + (ore * hi + oim * hr)
        else:
            sr, si = re * kr - im * ki, re * ki + im * kr
        spectrum = jnp.concatenate([sr, si], axis=0)
        high, low = split_value(spectrum)
        pieces[r] = dot(ih_ref[u], high) + dot(ih_ref[u], low) + dot(il_ref[u], high)

    if special:
        @pl.when(now < steps)
        def _():
            for u in range(share):
                waves[now * share + u] = wave(now * share + u, u)

        @pl.when(now >= steps)
        def _():
            for u in range(share):
                r = (now - steps) * share + u
                finish(r, u, waves[r])
    else:
        for u in range(share):
            r = now * share + u
            finish(r, u, wave(r, u))

    def backward(b, carry):
        at = pl.ds(pl.multiple_of(b * 8, 8), 8)
        also = pl.ds(pl.multiple_of(INNER + b * 8, 8), 8)
        values = [(pieces[r, at, :], pieces[r, also, :]) for r in range(RADIX)]
        for n, (re, im) in enumerate(transform(values, 1)):
            x = n * INNER + b * 8
            pencil = x // (out_rows * depths)
            depth = lax.rem(x // out_rows - mine + depths, depths)
            put = pl.ds(pl.multiple_of(lax.rem(x, out_rows), 8), 8)
            out_ref[depth, pencil, 0, put, :] = re
            out_ref[depth, pencil, 1, put, :] = im
        return carry

    @pl.when(now == pl.num_programs(0) - 1)
    def _():
        lax.fori_loop(0, INNER // 8, backward, 0)


def fields_kernel(pencils, width, *refs):
    chunks = RADIX // pencils // width
    ins, (high_ref, low_ref, out_ref, pieces) = refs[:chunks], refs[chunks:]
    per = RADIX // pencils
    rows = out_ref.shape[1]

    def pair(t):
        if width == 2:
            pencil, place = divmod(2 * t, per)
            ref = ins[place // 2]
            return jnp.concatenate([ref[pencil, 0], ref[pencil, 1]], axis=1)
        found = []
        for c in range(2):
            for odd in range(2):
                pencil, place = divmod(2 * t + odd, per)
                found.append(ins[place][pencil, c])
        return jnp.concatenate(found, axis=1)

    for s in range(8):
        total = None
        for place, r in enumerate((s, 8 if s == 0 else RADIX - s)):
            high, low = split_value(pair(r // 2))
            table_high = high_ref[s, 256 * place : 256 * place + 256]
            table_low = low_ref[s, 256 * place : 256 * place + 256]
            part = dot(high, table_high) + dot(low, table_high) + dot(high, table_low)
            total = part if total is None else total + part
        pieces[s] = total

    def step(b, carry):
        at = pl.ds(pl.multiple_of(b * 8, 8), 8)
        values = [(pieces[0, at, :INNER], None)]
        for s in range(1, 8):
            values.append((pieces[s, at, :INNER], pieces[s, at, INNER:]))
        values.append((pieces[0, at, INNER:], None))
        for n, value in enumerate(real_inverse(values)):
            out_ref[0, at, n * INNER : (n + 1) * INNER] = value
        return carry

    lax.fori_loop(0, rows // 8, step, 0)


def params(**more):
    return pltpu.CompilerParams(vmem_limit_bytes=48 * 1024 * 1024, **more)


def body(density, background, member_ids, layer_kernel, kernel_spectra):
    pencils = lax.axis_size("pencil")
    depths = lax.axis_size("depth")
    sharers = lax.axis_size("grp") * lax.axis_size("mem")
    pencil = lax.axis_index("pencil")
    per = RADIX // pencils
    width = min(per, 2)
    chunks = per // width
    lanes = width * HALF
    part_rows = density.shape[2]
    out_rows = part_rows // depths
    vmem = pl.BlockSpec(memory_space=pltpu.VMEM)
    smem = pl.BlockSpec(memory_space=pltpu.SMEM)

    kern_count = kernel_spectra.shape[0]
    local = layer_kernel[0] - lax.axis_index("depth") * kern_count
    share = RADIX // sharers
    first = lax.axis_index(("grp", "mem")) * share
    index = np.arange(INNER)
    swaps = np.zeros((2, INNER, INNER), np.float32)
    swaps[0, index, (INNER - index) % INNER] = 1.0
    swaps[1, index, INNER - 1 - index] = 1.0
    turns = jnp.asarray(swaps.transpose(0, 2, 1)[:, :, :HALF].astype(bf16))
    swaps = jnp.asarray(swaps.astype(bf16))
    groups = [1] if per == 1 else [1, per - 1]
    moved = pl.pallas_call(
        mirror_kernel,
        grid_spec=pltpu.PrefetchScalarGridSpec(
            num_scalar_prefetch=1,
            grid=(share,),
            in_specs=[
                pl.BlockSpec(
                    (None, 2, INNER, per * INNER), lambda i, w: (w[0], 0, lax.rem(RADIX - w[1] - i, RADIX), 0)
                ),
                pl.BlockSpec((2, INNER, INNER), lambda i, w: (0, 0, 0)),
                pl.BlockSpec((2, INNER, HALF), lambda i, w: (0, 0, 0)),
            ],
            out_specs=[pl.BlockSpec((g, 1, INNER, INNER), lambda i, w: (0, i, 0, 0)) for g in groups],
        ),
        out_shape=[jax.ShapeDtypeStruct((g, share, INNER, INNER), f32) for g in groups],
        compiler_params=params(),
        cost_estimate=pl.CostEstimate(flops=1 << 20, bytes_accessed=2 << 20, transcendentals=0),
    )(jnp.stack([local, first, pencil]), kernel_spectra, swaps, turns)
    mirrored = lax.ppermute(moved[0], "pencil", [(p, (pencils - p) % pencils) for p in range(pencils)])
    if per > 1:
        rest = lax.ppermute(moved[1], "pencil", [(p, pencils - 1 - p) for p in range(pencils)])

    offset = lax.dynamic_index_in_dim(background[:, 0], member_ids[0], 0, keepdims=True)
    row_high, row_low = halves(row_tables())
    block = min(part_rows, 128)
    sent = pl.pallas_call(
        functools.partial(rows_kernel, pencils, width),
        grid=(part_rows // block,),
        in_specs=[
            smem,
            pl.BlockSpec((None, None, block, LENGTH), lambda i: (0, 0, i, 0)),
            pl.BlockSpec((8, 512, 256), lambda i: (0, 0, 0)),
            pl.BlockSpec((8, 512, 256), lambda i: (0, 0, 0)),
        ],
        out_specs=[pl.BlockSpec((pencils, 2, block, lanes), lambda i: (0, 0, i, 0))] * chunks,
        out_shape=[jax.ShapeDtypeStruct((pencils, 2, part_rows, lanes), f32)] * chunks,
        scratch_shapes=[pltpu.VMEM((8, block, 256), f32)],
        compiler_params=params(),
        cost_estimate=pl.CostEstimate(flops=6 * part_rows * 2 * LENGTH * 512, bytes_accessed=12 << 20, transcendentals=0),
    )(offset, density, row_high, row_low)
    arrived = [lax.all_to_all(part, "pencil", 0, 0, tiled=True) for part in sent]
    if per > 1:
        mirrored = jnp.concatenate([mirrored, rest], axis=0)
    mirrored, _ = lax.optimization_barrier((mirrored, sent[0]))
    mirrored = lax.all_gather(mirrored, ("grp", "mem"), axis=0)

    sign = jnp.array([0.5, -0.5], f32)
    edge = lax.dynamic_slice(kernel_spectra, (local, 0, 0, HALF), (1, 2, LENGTH, 1))
    edge = edge.reshape(2, RADIX, INNER).astype(f32)
    flipped = jnp.concatenate([edge[:, :1], edge[:, :0:-1]], axis=1)[..., ::-1]
    flipped = jnp.concatenate([jnp.roll(flipped[:, :1], 1, axis=2), flipped[:, 1:]], axis=1)
    edge = 0.5 * edge + sign.reshape(2, 1, 1) * flipped
    edge = jnp.where(lax.broadcasted_iota(jnp.int32, (lanes,), 0) == 0, edge[..., None], 0.0)

    column = column_tables()
    tables = halves(column) + halves(column.transpose(0, 2, 1))
    pick = np.zeros((width * INNER, lanes), np.float32)
    for j in range(width):
        pick[j * INNER + np.arange(HALF), j * HALF + np.arange(HALF)] = 0.5
    pick = jnp.asarray(pick.astype(bf16))
    two = depths == 2
    mine = lax.axis_index("depth") if two else jnp.int32(0)
    where = jnp.stack([mine, local, pencil])
    fields = []
    before = None
    for k in range(chunks):
        special = k == 0
        steps = sharers

        def early(i, special=special):
            return jnp.minimum(i, steps - 1) if special else i

        def late(i, special=special):
            return jnp.maximum(i - steps, 0) if special else i

        here = arrived[k]
        if before is not None:
            here, before = lax.optimization_barrier((here, before))
            fields.append(lax.all_to_all(before, "pencil", 0, 0, tiled=True))
        edge_block = (2, share, INNER, lanes) if special else (2, 1, 8, lanes)
        out = pl.pallas_call(
            functools.partial(columns_kernel, special),
            grid_spec=pltpu.PrefetchScalarGridSpec(
                num_scalar_prefetch=1,
                grid=(2 * steps if special else steps,),
                in_specs=[
                    pl.BlockSpec((pencils, 2, part_rows, lanes), lambda i, w: (0, 0, 0, 0)),
                    pl.BlockSpec(
                        (None, 2, share * INNER, width * INNER), lambda i, w, k=k, late=late: (w[1], 0, late(i), k)
                    ),
                    pl.BlockSpec(
                        (None, width, share, INNER, INNER), lambda i, w, k=k, late=late: (late(i), k, 0, 0, 0)
                    ),
                    pl.BlockSpec(
                        edge_block,
                        (lambda i, w, late=late: (0, late(i), 0, 0)) if special else (lambda i, w: (0, 0, 0, 0)),
                    ),
                    pl.BlockSpec((2, INNER, INNER), lambda i, w: (0, 0, 0)),
                    pl.BlockSpec(pick.shape, lambda i, w: (0, 0)),
                ]
                + [pl.BlockSpec((share, 256, 256), lambda i, w, early=early: (early(i), 0, 0))] * 2
                + [pl.BlockSpec((share, 256, 256), lambda i, w, late=late: (late(i), 0, 0))] * 2,
                out_specs=pl.BlockSpec((depths, pencils, 2, out_rows, lanes), lambda i, w: (0, 0, 0, 0, 0)),
                scratch_shapes=[
                    pltpu.VMEM((RADIX, 256, lanes), f32),
                    pltpu.VMEM((RADIX if special else 1, 256, lanes), f32),
                ],
            ),
            out_shape=jax.ShapeDtypeStruct((depths, pencils, 2, out_rows, lanes), f32),
            compiler_params=params(),
            cost_estimate=pl.CostEstimate(
                flops=12 * RADIX * 256 * 256 * lanes, bytes_accessed=16 << 20, transcendentals=0
            ),
        )(where, here, kernel_spectra, mirrored, edge, swaps, pick, *tables)
        if two:
            before = out[0] + lax.ppermute(out[1], "depth", [(0, 1), (1, 0)])
        else:
            before = lax.psum_scatter(out, "depth", scatter_dimension=0, tiled=False)
    fields.append(lax.all_to_all(before, "pencil", 0, 0, tiled=True))

    back_high, back_low = halves(inverse_row_tables())
    return pl.pallas_call(
        functools.partial(fields_kernel, pencils, width),
        in_specs=[vmem] * (chunks + 2),
        out_specs=vmem,
        out_shape=jax.ShapeDtypeStruct((1, out_rows, LENGTH), f32),
        scratch_shapes=[pltpu.VMEM((8, out_rows, 256), f32)],
        compiler_params=params(),
        cost_estimate=pl.CostEstimate(flops=6 * out_rows * 2 * LENGTH * 512, bytes_accessed=8 << 20, transcendentals=0),
    )(*fields, back_high, back_low)


def solution(mesh):
    placed = (
        P(("grp", "mem"), "depth", "pencil", None),
        P(None, "depth"),
        P(("grp", "mem")),
        P("depth"),
        P("depth", None, None, "pencil"),
    )
    return jax.shard_map(
        body,
        mesh=mesh,
        in_specs=placed,
        out_specs=P(("grp", "mem"), ("pencil", "depth"), None),
        check_vma=False,
    )
```

```python
import functools
import math

import jax
import jax.numpy as jnp
import numpy as np
from jax import lax
from jax.experimental import pallas as pl
from jax.experimental.pallas import tpu as pltpu
from jax.sharding import PartitionSpec as P

RADIX = 16
INNER = 128
HALF = 64
LENGTH = RADIX * INNER
f32 = jnp.float32
bf16 = jnp.bfloat16


def halves(table):
    table = np.asarray(table, np.float32)
    high = table.astype(bf16)
    low = (table - high.astype(np.float32)).astype(bf16)
    return jnp.asarray(high), jnp.asarray(low)


def residue_rows(r):
    m = np.arange(INNER)[:, None]
    q = np.arange(HALF)[None, :]
    turn = np.exp(-2j * np.pi * (((RADIX * q + r) * m) % LENGTH) / LENGTH)
    re, im = turn.real.copy(), turn.imag.copy()
    if r == 0:
        im[:, 0] = (-1.0) ** m[:, 0]
    out = np.zeros((2 * INNER, 2 * HALF))
    if r == 0:
        out[:INNER, :HALF], out[:INNER, HALF:] = re, im
    elif r == 8:
        out[INNER:, :HALF], out[INNER:, HALF:] = re, im
    else:
        sign = 1.0 if r < 8 else -1.0
        out[:INNER, :HALF], out[:INNER, HALF:] = re, im
        out[INNER:, :HALF], out[INNER:, HALF:] = -sign * im, sign * re
    return out


def slot_of(r):
    return 0 if r in (0, 8) else min(r, RADIX - r)


def row_tables():
    tables = np.zeros((8, 512, 256))
    for t in range(8):
        for odd in range(2):
            block = residue_rows(2 * t + odd)
            rows = slice(256 * odd, 256 * odd + 256)
            tables[t, rows, HALF * odd : HALF * odd + HALF] = block[:, :HALF]
            tables[t, rows, 128 + HALF * odd : 128 + HALF * odd + HALF] = block[:, HALF:]
    return tables


def inverse_row_tables():
    tables = np.zeros((8, 512, 256))
    scale = 1.0 / (LENGTH * LENGTH)
    for s in range(8):
        for place, r in enumerate((s, 8 if s == 0 else RADIX - s)):
            block = residue_rows(r).T.copy() * scale
            weight = np.full((2 * HALF, 1), 2.0 if r in (0, 8) else 1.0)
            if r == 0:
                weight[0] = weight[HALF] = 1.0
            block *= weight
            odd = r % 2
            tables[s, 256 * place + HALF * odd : 256 * place + HALF * odd + HALF] += block[:HALF]
            tables[s, 256 * place + 128 + HALF * odd : 256 * place + 128 + HALF * odd + HALF] += block[HALF:]
    return tables


def column_tables():
    q = np.arange(INNER)[:, None]
    m = np.arange(INNER)[None, :]
    turn = np.exp(-2j * np.pi * ((q * m) % INNER) / INNER)
    table = np.block([[turn.real, -turn.imag], [turn.imag, turn.real]])
    angles = 2 * np.pi * np.arange(RADIX)[:, None] * np.arange(INNER)[None, :] / LENGTH
    turns = np.zeros((RADIX, INNER, INNER), np.float32)
    turns[..., 0] = np.cos(angles)
    turns[..., 1] = np.sin(angles)
    return table, turns


def split_value(value):
    high = value.astype(bf16)
    return high, (value - high.astype(f32)).astype(bf16)


def dot(a, b):
    return jnp.dot(a, b, preferred_element_type=f32)


def rotate(value, count, length, sign):
    re, im = value
    count %= length
    if count == 0:
        return value
    if 4 * count == length:
        return (im, -re) if sign < 0 else (-im, re)
    c = math.cos(2 * math.pi * count / length)
    s = sign * math.sin(2 * math.pi * count / length)
    if 8 * count == length:
        return ((re + im) * c, (im - re) * c) if sign < 0 else ((re - im) * c, (im + re) * c)
    return (re * c - im * s, re * s + im * c)


def plus(a, b):
    return (a[0] + b[0], a[1] + b[1])


def minus(a, b):
    return (a[0] - b[0], a[1] - b[1])


def transform(values, sign):
    length = len(values)
    if length == 1:
        return values
    even, odd = transform(values[0::2], sign), transform(values[1::2], sign)
    turned = [rotate(odd[k], k, length, sign) for k in range(length // 2)]
    return [plus(even[k], turned[k]) for k in range(length // 2)] + [
        minus(even[k], turned[k]) for k in range(length // 2)
    ]


def real_transform(values):
    length = len(values)
    if length == 2:
        return [(values[0] + values[1], None), (values[0] - values[1], None)]
    even, odd = real_transform(values[0::2]), real_transform(values[1::2])
    out = [None] * (length // 2 + 1)
    out[0] = (even[0][0] + odd[0][0], None)
    out[length // 2] = (even[0][0] - odd[0][0], None)
    quarter = length // 4
    for k in range(1, quarter):
        turned = rotate(odd[k], k, length, -1)
        out[k] = plus(even[k], turned)
        low = minus(even[k], turned)
        out[length // 2 - k] = (low[0], -low[1])
    out[quarter] = (even[quarter][0], -odd[quarter][0])
    return out


def real_inverse(values):
    half = len(values) - 1
    length = 2 * half
    if length == 2:
        return [values[0][0] + values[1][0], values[0][0] - values[1][0]]
    even, odd = [], []
    for k in range(half // 2 + 1):
        if k == 0:
            even.append((values[0][0] + values[half][0], None))
            odd.append((values[0][0] - values[half][0], None))
        elif k == half // 2:
            even.append((2.0 * values[k][0], None))
            odd.append((-2.0 * values[k][1], None))
        else:
            other = values[half - k]
            even.append((values[k][0] + other[0], values[k][1] - other[1]))
            odd.append(rotate((values[k][0] - other[0], values[k][1] + other[1]), k, length, 1))
    first, second = real_inverse(even), real_inverse(odd)
    return [x for pair in zip(first, second) for x in pair]


def rows_kernel(pencils, width, offset_ref, in_ref, high_ref, low_ref, *rest):
    outs, pieces = rest[:-1], rest[-1]
    rows = in_ref.shape[0]
    per = RADIX // pencils
    offset = offset_ref[0]

    def step(b, carry):
        at = pl.ds(pl.multiple_of(b * 8, 8), 8)
        values = [in_ref[at, n * INNER : (n + 1) * INNER] - offset for n in range(RADIX)]
        got = real_transform(values)
        pieces[0, at, :INNER] = got[0][0]
        pieces[0, at, INNER:] = got[8][0]
        for s in range(1, 8):
            pieces[s, at, :INNER] = got[s][0]
            pieces[s, at, INNER:] = got[s][1]
        return carry

    lax.fori_loop(0, rows // 8, step, 0)
    for t in range(8):
        total = None
        for odd in range(2):
            high, low = split_value(pieces[slot_of(2 * t + odd)])
            table_high = high_ref[t, 256 * odd : 256 * odd + 256]
            table_low = low_ref[t, 256 * odd : 256 * odd + 256]
            part = dot(high, table_high) + dot(low, table_high) + dot(high, table_low)
            total = part if total is None else total + part
        if width == 2:
            pencil, place = divmod(2 * t, per)
            for c in range(2):
                outs[place // 2][pencil, c] = total[:, c * 128 : (c + 1) * 128]
        else:
            for odd in range(2):
                pencil, place = divmod(2 * t + odd, per)
                for c in range(2):
                    begin = c * 128 + odd * HALF
                    outs[place][pencil, c] = total[:, begin : begin + HALF]


def mirror_kernel(where_ref, in_ref, zero_ref, *rest_refs):
    per = in_ref.shape[2] // INNER

    def swapped(zero, shape, axis):
        to = lax.broadcasted_iota(jnp.int32, shape, axis)
        begin = lax.broadcasted_iota(jnp.int32, shape, 1 - axis)
        total = jnp.where(zero, INNER, INNER - 1)
        return jnp.where((to + begin == total) | (zero & (to + begin == 0)), 1.0, 0.0).astype(bf16)

    swap = swapped(where_ref[1] + pl.program_id(0) == 0, (INNER, INNER), 0)
    plain = swapped(where_ref[1] < 0, (INNER, HALF), 1)
    for j in range(per):
        turn = swapped(where_ref[2] == 0, (INNER, HALF), 1) if j == 0 else plain
        turned = [dot(in_ref[c, :, j * INNER : (j + 1) * INNER], turn) for c in range(2)]
        value = dot(swap, jnp.concatenate(turned, axis=1).astype(bf16))
        if j == 0:
            zero_ref[0, 0] = value
        else:
            rest_refs[0][per - 1 - j, 0] = value


def columns_kernel(special, where_ref, in_ref, kern_ref, mirror_ref, edge_ref, swap_ref, pick_ref,
                   turns_ref, late_ref, fh_ref, fl_ref, ih_ref, il_ref, out_ref, pieces, waves):
    part_rows = in_ref.shape[2]
    depths, splits, pencils, _, split_rows, lanes = out_ref.shape
    out_rows = splits * split_rows
    share = mirror_ref.shape[1]
    steps = RADIX // share
    mine = where_ref[0]
    now = pl.program_id(0)

    def forward(b, carry):
        values = []
        for n in range(RADIX):
            source, begin = divmod(n * INNER, part_rows)
            at = pl.ds(pl.multiple_of(begin + b * 8, 8), 8)
            values.append((in_ref[source, 0, at, :], in_ref[source, 1, at, :]))
        at = pl.ds(pl.multiple_of(b * 8, 8), 8)
        also = pl.ds(pl.multiple_of(INNER + b * 8, 8), 8)
        for r, (re, im) in enumerate(transform(values, -1)):
            pieces[r, at, :] = re
            pieces[r, also, :] = im
        return carry

    @pl.when(now == 0)
    def _():
        lax.fori_loop(0, INNER // 8, forward, 0)

    def wave(r, u):
        re, im = pieces[r, :INNER], pieces[r, INNER:]
        c, s = turns_ref[u, :, 0:1], turns_ref[u, :, 1:2]
        high, low = split_value(jnp.concatenate([re * c + im * s, im * c - re * s], axis=0))
        return dot(fh_ref[...], high) + dot(fh_ref[...], low) + dot(fl_ref[...], high)

    def finish(r, u, got):
        re, im = got[:INNER], got[INNER:]
        tiles = [mirror_ref[j, u] for j in range(mirror_ref.shape[0])]
        rows = slice(u * INNER, (u + 1) * INNER)
        parts = []
        for c in range(2):
            other = [tile[:, c * HALF : (c + 1) * HALF] for tile in tiles]
            other = jnp.concatenate(other, axis=1) if len(other) > 1 else other[0]
            own = dot(kern_ref[c, rows, :], pick_ref[...])
            parts.append(own + 0.5 * other if c == 0 else own - 0.5 * other)
        kr, ki = parts
        if special:
            other = lax.rem(RADIX - r, RADIX)
            high, low = split_value(waves[other])
            swap = swap_ref[jnp.where(r == 0, 0, 1)]
            ore = dot(swap, high[:INNER]) + dot(swap, low[:INNER])
            oim = -(dot(swap, high[INNER:]) + dot(swap, low[INNER:]))
            mask = (lax.broadcasted_iota(jnp.int32, (INNER, lanes), 1) == 0) & (where_ref[2] == 0)
            hr = jnp.where(mask, 0.5 * (kr - edge_ref[0, u]), 0.0)
            hi = jnp.where(mask, 0.5 * (ki - edge_ref[1, u]), 0.0)
            kr, ki = kr - hr, ki - hi
            sr = re * kr - im * ki + (ore * hr - oim * hi)
            si = re * ki + im * kr + (ore * hi + oim * hr)
        else:
            sr, si = re * kr - im * ki, re * ki + im * kr
        spectrum = jnp.concatenate([sr, si], axis=0)
        high, low = split_value(spectrum)
        got = dot(ih_ref[...], high) + dot(ih_ref[...], low) + dot(il_ref[...], high)
        re, im = got[:INNER], got[INNER:]
        c, s = late_ref[u, :, 0:1], late_ref[u, :, 1:2]
        pieces[r, :INNER] = re * c - im * s
        pieces[r, INNER:] = im * c + re * s

    if special:
        @pl.when(now < steps)
        def _():
            for u in range(share):
                waves[now * share + u] = wave(now * share + u, u)

        @pl.when(now >= steps)
        def _():
            for u in range(share):
                r = (now - steps) * share + u
                finish(r, u, waves[r])
    else:
        for u in range(share):
            r = now * share + u
            finish(r, u, wave(r, u))

    def backward(b, carry):
        at = pl.ds(pl.multiple_of(b * 8, 8), 8)
        also = pl.ds(pl.multiple_of(INNER + b * 8, 8), 8)
        values = [(pieces[r, at, :], pieces[r, also, :]) for r in range(RADIX)]
        for n, (re, im) in enumerate(transform(values, 1)):
            x = n * INNER + b * 8
            pencil = x // (out_rows * depths)
            depth = lax.rem(x // out_rows - mine + depths, depths)
            part = lax.rem(x, out_rows) // split_rows
            put = pl.ds(pl.multiple_of(lax.rem(x, split_rows), 8), 8)
            out_ref[depth, part, pencil, 0, put, :] = re
            out_ref[depth, part, pencil, 1, put, :] = im
        return carry

    @pl.when(now == pl.num_programs(0) - 1)
    def _():
        lax.fori_loop(0, INNER // 8, backward, 0)


def fields_kernel(pencils, width, counts, *refs):
    ins, at = [], 0
    for count in counts:
        ins.append(refs[at : at + count])
        at += count
    high_ref, low_ref, out_ref, pieces = refs[at:]
    per = RADIX // pencils
    rows = out_ref.shape[1]

    def read(chunk, pencil, c):
        found = [ref[pencil, c] for ref in ins[chunk]]
        return jnp.concatenate(found, axis=0) if len(found) > 1 else found[0]

    def pair(t):
        if width == 2:
            pencil, place = divmod(2 * t, per)
            return jnp.concatenate([read(place // 2, pencil, c) for c in range(2)], axis=1)
        found = []
        for c in range(2):
            for odd in range(2):
                pencil, place = divmod(2 * t + odd, per)
                found.append(read(place, pencil, c))
        return jnp.concatenate(found, axis=1)

    for s in range(8):
        total = None
        for place, r in enumerate((s, 8 if s == 0 else RADIX - s)):
            high, low = split_value(pair(r // 2))
            table_high = high_ref[s, 256 * place : 256 * place + 256]
            table_low = low_ref[s, 256 * place : 256 * place + 256]
            part = dot(high, table_high) + dot(low, table_high) + dot(high, table_low)
            total = part if total is None else total + part
        pieces[s] = total

    def step(b, carry):
        at = pl.ds(pl.multiple_of(b * 8, 8), 8)
        values = [(pieces[0, at, :INNER], None)]
        for s in range(1, 8):
            values.append((pieces[s, at, :INNER], pieces[s, at, INNER:]))
        values.append((pieces[0, at, INNER:], None))
        for n, value in enumerate(real_inverse(values)):
            out_ref[0, at, n * INNER : (n + 1) * INNER] = value
        return carry

    lax.fori_loop(0, rows // 8, step, 0)


def params(**more):
    return pltpu.CompilerParams(vmem_limit_bytes=48 * 1024 * 1024, **more)


def body(density, background, member_ids, layer_kernel, kernel_spectra):
    pencils = lax.axis_size("pencil")
    depths = lax.axis_size("depth")
    sharers = lax.axis_size("grp") * lax.axis_size("mem")
    pencil = lax.axis_index("pencil")
    per = RADIX // pencils
    width = min(per, 2)
    chunks = per // width
    lanes = width * HALF
    part_rows = density.shape[2]
    out_rows = part_rows // depths
    vmem = pl.BlockSpec(memory_space=pltpu.VMEM)
    smem = pl.BlockSpec(memory_space=pltpu.SMEM)

    kern_count = kernel_spectra.shape[0]
    local = layer_kernel[0] - lax.axis_index("depth") * kern_count
    share = RADIX // sharers
    first = lax.axis_index(("grp", "mem")) * share
    index = np.arange(INNER)
    swaps = np.zeros((2, INNER, INNER), np.float32)
    swaps[0, index, (INNER - index) % INNER] = 1.0
    swaps[1, index, INNER - 1 - index] = 1.0
    swaps = jnp.asarray(swaps.astype(bf16))
    groups = [1] if per == 1 else [1, per - 1]
    moved = pl.pallas_call(
        mirror_kernel,
        grid_spec=pltpu.PrefetchScalarGridSpec(
            num_scalar_prefetch=1,
            grid=(share,),
            in_specs=[
                pl.BlockSpec(
                    (None, 2, INNER, per * INNER), lambda i, w: (w[0], 0, lax.rem(RADIX - w[1] - i, RADIX), 0)
                ),
            ],
            out_specs=[pl.BlockSpec((g, 1, INNER, INNER), lambda i, w: (0, i, 0, 0)) for g in groups],
        ),
        out_shape=[jax.ShapeDtypeStruct((g, share, INNER, INNER), f32) for g in groups],
        compiler_params=params(),
        cost_estimate=pl.CostEstimate(flops=1 << 20, bytes_accessed=2 << 20, transcendentals=0),
    )(jnp.stack([local, first, pencil]), kernel_spectra)
    mirrored = lax.ppermute(moved[0], "pencil", [(p, (pencils - p) % pencils) for p in range(pencils)])
    if per > 1:
        rest = lax.ppermute(moved[1], "pencil", [(p, pencils - 1 - p) for p in range(pencils)])

    offset = lax.dynamic_index_in_dim(background[:, 0], member_ids[0], 0, keepdims=True)
    row_high, row_low = halves(row_tables())
    block = min(part_rows, 128)
    sent = pl.pallas_call(
        functools.partial(rows_kernel, pencils, width),
        grid=(part_rows // block,),
        in_specs=[
            smem,
            pl.BlockSpec((None, None, block, LENGTH), lambda i: (0, 0, i, 0)),
            pl.BlockSpec((8, 512, 256), lambda i: (0, 0, 0)),
            pl.BlockSpec((8, 512, 256), lambda i: (0, 0, 0)),
        ],
        out_specs=[pl.BlockSpec((pencils, 2, block, lanes), lambda i: (0, 0, i, 0))] * chunks,
        out_shape=[jax.ShapeDtypeStruct((pencils, 2, part_rows, lanes), f32)] * chunks,
        scratch_shapes=[pltpu.VMEM((8, block, 256), f32)],
        compiler_params=params(),
        cost_estimate=pl.CostEstimate(flops=6 * part_rows * 2 * LENGTH * 512, bytes_accessed=12 << 20, transcendentals=0),
    )(offset, density, row_high, row_low)
    arrived = [lax.all_to_all(part, "pencil", 0, 0, tiled=True) for part in sent]

    sign = jnp.array([0.5, -0.5], f32)
    edge = lax.dynamic_slice(kernel_spectra, (local, 0, 0, HALF), (1, 2, LENGTH, 1))
    edge = edge.reshape(2, RADIX, INNER).astype(f32)
    flipped = jnp.concatenate([edge[:, :1], edge[:, :0:-1]], axis=1)[..., ::-1]
    flipped = jnp.concatenate([jnp.roll(flipped[:, :1], 1, axis=2), flipped[:, 1:]], axis=1)
    edge = 0.5 * edge + sign.reshape(2, 1, 1) * flipped
    edge = jnp.where(lax.broadcasted_iota(jnp.int32, (lanes,), 0) == 0, edge[..., None], 0.0)

    if per > 1:
        mirrored = jnp.concatenate([mirrored, rest], axis=0)
    mirrored, edge, _ = lax.optimization_barrier((mirrored, edge, sent[0]))
    mirrored = lax.all_gather(mirrored, ("grp", "mem"), axis=0)

    column, column_turns = column_tables()
    column_turns = jnp.asarray(column_turns)
    tables = halves(column) + halves(column.T)
    pick = np.zeros((width * INNER, lanes), np.float32)
    for j in range(width):
        pick[j * INNER + np.arange(HALF), j * HALF + np.arange(HALF)] = 0.5
    pick = jnp.asarray(pick.astype(bf16))
    two = depths == 2
    mine = lax.axis_index("depth") if two else jnp.int32(0)
    where = jnp.stack([mine, local, pencil])
    fields, counts = [], []
    before = None
    for k in range(chunks):
        special = k == 0
        steps = sharers

        def early(i, special=special):
            return jnp.minimum(i, steps - 1) if special else i

        def late(i, special=special):
            return jnp.maximum(i - steps, 0) if special else i

        here = arrived[k]
        splits = 2 if two and k == chunks - 1 else 1
        counts.append(splits)
        split_rows = out_rows // splits
        if before is not None:
            here, before = lax.optimization_barrier((here, before))
            fields.append(lax.all_to_all(before, "pencil", 0, 0, tiled=True))
        edge_block = (2, share, INNER, lanes) if special else (2, 1, 8, lanes)
        out = pl.pallas_call(
            functools.partial(columns_kernel, special),
            grid_spec=pltpu.PrefetchScalarGridSpec(
                num_scalar_prefetch=1,
                grid=(2 * steps if special else steps,),
                in_specs=[
                    pl.BlockSpec((pencils, 2, part_rows, lanes), lambda i, w: (0, 0, 0, 0)),
                    pl.BlockSpec(
                        (None, 2, share * INNER, width * INNER), lambda i, w, k=k, late=late: (w[1], 0, late(i), k)
                    ),
                    pl.BlockSpec(
                        (None, width, share, INNER, INNER), lambda i, w, k=k, late=late: (late(i), k, 0, 0, 0)
                    ),
                    pl.BlockSpec(
                        edge_block,
                        (lambda i, w, late=late: (0, late(i), 0, 0)) if special else (lambda i, w: (0, 0, 0, 0)),
                    ),
                    pl.BlockSpec((2, INNER, INNER), lambda i, w: (0, 0, 0)),
                    pl.BlockSpec(pick.shape, lambda i, w: (0, 0)),
                ]
                + [pl.BlockSpec((share, INNER, INNER), lambda i, w, early=early: (early(i), 0, 0))]
                + [pl.BlockSpec((share, INNER, INNER), lambda i, w, late=late: (late(i), 0, 0))]
                + [pl.BlockSpec((256, 256), lambda i, w: (0, 0))] * 4,
                out_specs=pl.BlockSpec(
                    (depths, splits, pencils, 2, split_rows, lanes), lambda i, w: (0, 0, 0, 0, 0, 0)
                ),
                scratch_shapes=[
                    pltpu.VMEM((RADIX, 256, lanes), f32),
                    pltpu.VMEM((RADIX if special else 1, 256, lanes), f32),
                ],
            ),
            out_shape=jax.ShapeDtypeStruct((depths, splits, pencils, 2, split_rows, lanes), f32),
            compiler_params=params(),
            cost_estimate=pl.CostEstimate(
                flops=12 * RADIX * 256 * 256 * lanes, bytes_accessed=16 << 20, transcendentals=0
            ),
        )(where, here, kernel_spectra, mirrored, edge, swaps, pick, column_turns, column_turns, *tables)
        if not two:
            before = lax.psum_scatter(out[:, 0], "depth", scatter_dimension=0, tiled=False)
            continue
        before = out[0, 0] + lax.ppermute(out[1, 0], "depth", [(0, 1), (1, 0)])
        if splits == 2:
            second, before = lax.optimization_barrier((out[1, 1], before))
            fields.append(lax.all_to_all(before, "pencil", 0, 0, tiled=True))
            before = out[0, 1] + lax.ppermute(second, "depth", [(0, 1), (1, 0)])
    fields.append(lax.all_to_all(before, "pencil", 0, 0, tiled=True))

    back_high, back_low = halves(inverse_row_tables())
    return pl.pallas_call(
        functools.partial(fields_kernel, pencils, width, counts),
        in_specs=[vmem] * (len(fields) + 2),
        out_specs=vmem,
        out_shape=jax.ShapeDtypeStruct((1, out_rows, LENGTH), f32),
        scratch_shapes=[pltpu.VMEM((8, out_rows, 256), f32)],
        compiler_params=params(),
        cost_estimate=pl.CostEstimate(flops=6 * out_rows * 2 * LENGTH * 512, bytes_accessed=8 << 20, transcendentals=0),
    )(*fields, back_high, back_low)


def solution(mesh):
    placed = (
        P(("grp", "mem"), "depth", "pencil", None),
        P(None, "depth"),
        P(("grp", "mem")),
        P("depth"),
        P("depth", None, None, "pencil"),
    )
    return jax.shard_map(
        body,
        mesh=mesh,
        in_specs=placed,
        out_specs=P(("grp", "mem"), ("pencil", "depth"), None),
        check_vma=False,
    )
```

```python
import functools
import math

import jax
import jax.numpy as jnp
import numpy as np
from jax import lax
from jax.experimental import pallas as pl
from jax.experimental.pallas import tpu as pltpu
from jax.sharding import PartitionSpec as P

RADIX = 16
INNER = 128
HALF = 64
LENGTH = RADIX * INNER
f32 = jnp.float32
bf16 = jnp.bfloat16


def halves(table):
    table = np.asarray(table, np.float32)
    high = table.astype(bf16)
    low = (table - high.astype(np.float32)).astype(bf16)
    return jnp.asarray(high), jnp.asarray(low)


def residue_rows(r):
    m = np.arange(INNER)[:, None]
    q = np.arange(HALF)[None, :]
    turn = np.exp(-2j * np.pi * (((RADIX * q + r) * m) % LENGTH) / LENGTH)
    re, im = turn.real.copy(), turn.imag.copy()
    if r == 0:
        im[:, 0] = (-1.0) ** m[:, 0]
    out = np.zeros((2 * INNER, 2 * HALF))
    if r == 0:
        out[:INNER, :HALF], out[:INNER, HALF:] = re, im
    elif r == 8:
        out[INNER:, :HALF], out[INNER:, HALF:] = re, im
    else:
        sign = 1.0 if r < 8 else -1.0
        out[:INNER, :HALF], out[:INNER, HALF:] = re, im
        out[INNER:, :HALF], out[INNER:, HALF:] = -sign * im, sign * re
    return out


def slot_of(r):
    return 0 if r in (0, 8) else min(r, RADIX - r)


def row_tables():
    tables = np.zeros((8, 512, 256))
    for t in range(8):
        for odd in range(2):
            block = residue_rows(2 * t + odd)
            rows = slice(256 * odd, 256 * odd + 256)
            tables[t, rows, HALF * odd : HALF * odd + HALF] = block[:, :HALF]
            tables[t, rows, 128 + HALF * odd : 128 + HALF * odd + HALF] = block[:, HALF:]
    return tables


def inverse_row_tables():
    tables = np.zeros((8, 512, 256))
    scale = 1.0 / (LENGTH * LENGTH)
    for s in range(8):
        for place, r in enumerate((s, 8 if s == 0 else RADIX - s)):
            block = residue_rows(r).T.copy() * scale
            weight = np.full((2 * HALF, 1), 2.0 if r in (0, 8) else 1.0)
            if r == 0:
                weight[0] = weight[HALF] = 1.0
            block *= weight
            odd = r % 2
            tables[s, 256 * place + HALF * odd : 256 * place + HALF * odd + HALF] += block[:HALF]
            tables[s, 256 * place + 128 + HALF * odd : 256 * place + 128 + HALF * odd + HALF] += block[HALF:]
    return tables


def column_tables():
    q = np.arange(INNER)[:, None]
    m = np.arange(INNER)[None, :]
    turn = np.exp(-2j * np.pi * ((q * m) % INNER) / INNER)
    table = np.block([[turn.real, -turn.imag], [turn.imag, turn.real]])
    angles = 2 * np.pi * np.arange(RADIX)[:, None] * np.arange(INNER)[None, :] / LENGTH
    turns = np.zeros((RADIX, INNER, INNER), np.float32)
    turns[..., 0] = np.cos(angles)
    turns[..., 1] = np.sin(angles)
    return table, turns


def split_value(value):
    high = value.astype(bf16)
    return high, (value - high.astype(f32)).astype(bf16)


def dot(a, b):
    return jnp.dot(a, b, preferred_element_type=f32)


def rotate(value, count, length, sign):
    re, im = value
    count %= length
    if count == 0:
        return value
    if 4 * count == length:
        return (im, -re) if sign < 0 else (-im, re)
    c = math.cos(2 * math.pi * count / length)
    s = sign * math.sin(2 * math.pi * count / length)
    if 8 * count == length:
        return ((re + im) * c, (im - re) * c) if sign < 0 else ((re - im) * c, (im + re) * c)
    return (re * c - im * s, re * s + im * c)


def plus(a, b):
    return (a[0] + b[0], a[1] + b[1])


def minus(a, b):
    return (a[0] - b[0], a[1] - b[1])


def transform(values, sign):
    length = len(values)
    if length == 1:
        return values
    even, odd = transform(values[0::2], sign), transform(values[1::2], sign)
    turned = [rotate(odd[k], k, length, sign) for k in range(length // 2)]
    return [plus(even[k], turned[k]) for k in range(length // 2)] + [
        minus(even[k], turned[k]) for k in range(length // 2)
    ]


def real_transform(values):
    length = len(values)
    if length == 2:
        return [(values[0] + values[1], None), (values[0] - values[1], None)]
    even, odd = real_transform(values[0::2]), real_transform(values[1::2])
    out = [None] * (length // 2 + 1)
    out[0] = (even[0][0] + odd[0][0], None)
    out[length // 2] = (even[0][0] - odd[0][0], None)
    quarter = length // 4
    for k in range(1, quarter):
        turned = rotate(odd[k], k, length, -1)
        out[k] = plus(even[k], turned)
        low = minus(even[k], turned)
        out[length // 2 - k] = (low[0], -low[1])
    out[quarter] = (even[quarter][0], -odd[quarter][0])
    return out


def real_inverse(values):
    half = len(values) - 1
    length = 2 * half
    if length == 2:
        return [values[0][0] + values[1][0], values[0][0] - values[1][0]]
    even, odd = [], []
    for k in range(half // 2 + 1):
        if k == 0:
            even.append((values[0][0] + values[half][0], None))
            odd.append((values[0][0] - values[half][0], None))
        elif k == half // 2:
            even.append((2.0 * values[k][0], None))
            odd.append((-2.0 * values[k][1], None))
        else:
            other = values[half - k]
            even.append((values[k][0] + other[0], values[k][1] - other[1]))
            odd.append(rotate((values[k][0] - other[0], values[k][1] + other[1]), k, length, 1))
    first, second = real_inverse(even), real_inverse(odd)
    return [x for pair in zip(first, second) for x in pair]


def rows_kernel(pencils, width, offset_ref, in_ref, high_ref, low_ref, *rest):
    outs, pieces = rest[:-1], rest[-1]
    rows = in_ref.shape[0]
    per = RADIX // pencils
    offset = offset_ref[0]

    def step(b, carry):
        at = pl.ds(pl.multiple_of(b * 8, 8), 8)
        values = [in_ref[at, n * INNER : (n + 1) * INNER] - offset for n in range(RADIX)]
        got = real_transform(values)
        pieces[0, at, :INNER] = got[0][0]
        pieces[0, at, INNER:] = got[8][0]
        for s in range(1, 8):
            pieces[s, at, :INNER] = got[s][0]
            pieces[s, at, INNER:] = got[s][1]
        return carry

    lax.fori_loop(0, rows // 8, step, 0)
    for t in range(8):
        total = None
        for odd in range(2):
            high, low = split_value(pieces[slot_of(2 * t + odd)])
            table_high = high_ref[t, 256 * odd : 256 * odd + 256]
            table_low = low_ref[t, 256 * odd : 256 * odd + 256]
            part = dot(high, table_high) + dot(low, table_high) + dot(high, table_low)
            total = part if total is None else total + part
        if width == 2:
            pencil, place = divmod(2 * t, per)
            for c in range(2):
                outs[place // 2][pencil, c] = total[:, c * 128 : (c + 1) * 128]
        else:
            for odd in range(2):
                pencil, place = divmod(2 * t + odd, per)
                for c in range(2):
                    begin = c * 128 + odd * HALF
                    outs[place][pencil, c] = total[:, begin : begin + HALF]


def swapped(zero, shape, axis):
    total = lax.broadcasted_iota(jnp.int32, shape, 0) + lax.broadcasted_iota(jnp.int32, shape, 1)
    wanted = jnp.where(zero, INNER, INNER - 1)
    also = jnp.where(zero, 0, INNER - 1)
    return jnp.where((total == wanted) | (total == also), 1.0, 0.0).astype(bf16)


def mirror_kernel(share, where_ref, *refs):
    ins, zero_ref, rest_refs = refs[:share], refs[share], refs[share + 1 :]
    per = ins[0].shape[2] // INNER
    plain = swapped(where_ref[1] < 0, (INNER, HALF), 1)
    edge = swapped(where_ref[2] == 0, (INNER, HALF), 1)
    for u in range(share):
        swap = swapped(where_ref[1] + u == 0, (INNER, INNER), 0)
        for j in range(per):
            turn = edge if j == 0 else plain
            turned = [dot(ins[u][c, :, j * INNER : (j + 1) * INNER], turn) for c in range(2)]
            value = dot(swap, jnp.concatenate(turned, axis=1).astype(bf16))
            if j == 0:
                zero_ref[0, u] = value
            else:
                rest_refs[0][per - 1 - j, u] = value


def columns_kernel(special, where_ref, in_ref, kern_ref, mirror_ref, edge_ref,
                   turns_ref, late_ref, table_ref, out_ref, pieces, waves):
    part_rows = in_ref.shape[2]
    depths, pencils, _, out_rows, lanes = out_ref.shape
    share = mirror_ref.shape[1]
    steps = RADIX // share
    mine = where_ref[0]
    now = pl.program_id(0)
    from_lane = lax.broadcasted_iota(jnp.int32, (kern_ref.shape[2], lanes), 0)
    to_lane = lax.broadcasted_iota(jnp.int32, (kern_ref.shape[2], lanes), 1)
    wanted = to_lane + jnp.where(to_lane < HALF, 0, HALF)
    pick = jnp.where(from_lane == wanted, 0.5, 0.0).astype(bf16)
    zero_swap = swapped(mine >= 0, (INNER, INNER), 0)
    plain_swap = swapped(mine < 0, (INNER, INNER), 0)

    def forward(b, carry):
        values = []
        for n in range(RADIX):
            source, begin = divmod(n * INNER, part_rows)
            at = pl.ds(pl.multiple_of(begin + b * 8, 8), 8)
            values.append((in_ref[source, 0, at, :], in_ref[source, 1, at, :]))
        at = pl.ds(pl.multiple_of(b * 8, 8), 8)
        also = pl.ds(pl.multiple_of(INNER + b * 8, 8), 8)
        for r, (re, im) in enumerate(transform(values, -1)):
            pieces[r, at, :] = re
            pieces[r, also, :] = im
        return carry

    @pl.when(now == 0)
    def _():
        lax.fori_loop(0, INNER // 8, forward, 0)

    def wave(r, u):
        re, im = pieces[r, :INNER], pieces[r, INNER:]
        c, s = turns_ref[u, :, 0:1], turns_ref[u, :, 1:2]
        high, low = split_value(jnp.concatenate([re * c + im * s, im * c - re * s], axis=0))
        return dot(table_ref[0], high) + dot(table_ref[0], low) + dot(table_ref[1], high)

    def finish(r, u, got):
        re, im = got[:INNER], got[INNER:]
        tiles = [mirror_ref[j, u] for j in range(mirror_ref.shape[0])]
        rows = slice(u * INNER, (u + 1) * INNER)
        parts = []
        for c in range(2):
            other = [tile[:, c * HALF : (c + 1) * HALF] for tile in tiles]
            other = jnp.concatenate(other, axis=1) if len(other) > 1 else other[0]
            own = dot(kern_ref[c, rows, :], pick)
            parts.append(own + 0.5 * other if c == 0 else own - 0.5 * other)
        kr, ki = parts
        if special:
            other = lax.rem(RADIX - r, RADIX)
            high, low = split_value(waves[other])
            swap = jnp.where(r == 0, zero_swap.astype(f32), plain_swap.astype(f32)).astype(bf16) if u == 0 else plain_swap
            ore = dot(swap, high[:INNER]) + dot(swap, low[:INNER])
            oim = -(dot(swap, high[INNER:]) + dot(swap, low[INNER:]))
            mask = (lax.broadcasted_iota(jnp.int32, (INNER, lanes), 1) == 0) & (where_ref[2] == 0)
            hr = jnp.where(mask, 0.5 * (kr - edge_ref[0, u]), 0.0)
            hi = jnp.where(mask, 0.5 * (ki - edge_ref[1, u]), 0.0)
            kr, ki = kr - hr, ki - hi
            sr = re * kr - im * ki + (ore * hr - oim * hi)
            si = re * ki + im * kr + (ore * hi + oim * hr)
        else:
            sr, si = re * kr - im * ki, re * ki + im * kr
        spectrum = jnp.concatenate([sr, si], axis=0)
        high, low = split_value(spectrum)
        got = dot(table_ref[2], high) + dot(table_ref[2], low) + dot(table_ref[3], high)
        re, im = got[:INNER], got[INNER:]
        c, s = late_ref[u, :, 0:1], late_ref[u, :, 1:2]
        pieces[r, :INNER] = re * c - im * s
        pieces[r, INNER:] = im * c + re * s

    if special:
        @pl.when(now < steps)
        def _():
            for u in range(share):
                waves[now * share + u] = wave(now * share + u, u)

        @pl.when(now >= steps)
        def _():
            for u in range(share):
                r = (now - steps) * share + u
                finish(r, u, waves[r])
    else:
        for u in range(share):
            r = now * share + u
            finish(r, u, wave(r, u))

    slots = [lax.rem(d - mine + depths, depths) for d in range(depths)]

    def backward(b, carry):
        at = pl.ds(pl.multiple_of(b * 8, 8), 8)
        also = pl.ds(pl.multiple_of(INNER + b * 8, 8), 8)
        values = [(pieces[r, at, :], pieces[r, also, :]) for r in range(RADIX)]
        for n, (re, im) in enumerate(transform(values, 1)):
            if out_rows % INNER == 0:
                part, begin = divmod(n * INNER, out_rows)
                pencil, depth = divmod(part, depths)
                depth = slots[depth]
                put = pl.ds(pl.multiple_of(begin + b * 8, 8), 8)
            else:
                x = n * INNER + b * 8
                pencil = x // (out_rows * depths)
                depth = lax.rem(x // out_rows - mine + depths, depths)
                put = pl.ds(pl.multiple_of(lax.rem(x, out_rows), 8), 8)
            out_ref[depth, pencil, 0, put, :] = re
            out_ref[depth, pencil, 1, put, :] = im
        return carry

    @pl.when(now == pl.num_programs(0) - 1)
    def _():
        lax.fori_loop(0, INNER // 8, backward, 0)


def fields_kernel(pencils, width, counts, *refs):
    ins, at = [], 0
    for count in counts:
        ins.append(refs[at : at + count])
        at += count
    high_ref, low_ref, out_ref, pieces = refs[at:]
    per = RADIX // pencils
    rows = out_ref.shape[1]

    def read(chunk, pencil, c):
        found = [ref[pencil, c] for ref in ins[chunk]]
        return jnp.concatenate(found, axis=0) if len(found) > 1 else found[0]

    def pair(t):
        if width == 2:
            pencil, place = divmod(2 * t, per)
            return jnp.concatenate([read(place // 2, pencil, c) for c in range(2)], axis=1)
        found = []
        for c in range(2):
            for odd in range(2):
                pencil, place = divmod(2 * t + odd, per)
                found.append(read(place, pencil, c))
        return jnp.concatenate(found, axis=1)

    for s in range(8):
        total = None
        for place, r in enumerate((s, 8 if s == 0 else RADIX - s)):
            high, low = split_value(pair(r // 2))
            table_high = high_ref[s, 256 * place : 256 * place + 256]
            table_low = low_ref[s, 256 * place : 256 * place + 256]
            part = dot(high, table_high) + dot(low, table_high) + dot(high, table_low)
            total = part if total is None else total + part
        pieces[s] = total

    def step(b, carry):
        at = pl.ds(pl.multiple_of(b * 8, 8), 8)
        values = [(pieces[0, at, :INNER], None)]
        for s in range(1, 8):
            values.append((pieces[s, at, :INNER], pieces[s, at, INNER:]))
        values.append((pieces[0, at, INNER:], None))
        for n, value in enumerate(real_inverse(values)):
            out_ref[0, at, n * INNER : (n + 1) * INNER] = value
        return carry

    lax.fori_loop(0, rows // 8, step, 0)


def params(**more):
    return pltpu.CompilerParams(vmem_limit_bytes=48 * 1024 * 1024, **more)


def body(density, background, member_ids, layer_kernel, kernel_spectra):
    pencils = lax.axis_size("pencil")
    depths = lax.axis_size("depth")
    sharers = lax.axis_size("grp") * lax.axis_size("mem")
    pencil = lax.axis_index("pencil")
    per = RADIX // pencils
    width = min(per, 2)
    chunks = per // width
    lanes = width * HALF
    part_rows = density.shape[2]
    out_rows = part_rows // depths
    vmem = pl.BlockSpec(memory_space=pltpu.VMEM)
    smem = pl.BlockSpec(memory_space=pltpu.SMEM)

    kern_count = kernel_spectra.shape[0]
    local = layer_kernel[0] - lax.axis_index("depth") * kern_count
    share = RADIX // sharers
    first = lax.axis_index(("grp", "mem")) * share
    groups = [1] if per == 1 else [1, per - 1]
    moved = pl.pallas_call(
        functools.partial(mirror_kernel, share),
        grid_spec=pltpu.PrefetchScalarGridSpec(
            num_scalar_prefetch=1,
            grid=(1,),
            in_specs=[
                pl.BlockSpec(
                    (None, 2, INNER, per * INNER),
                    lambda i, w, u=u: (w[0], 0, lax.rem(RADIX - w[1] - u, RADIX), 0),
                )
                for u in range(share)
            ],
            out_specs=[pl.BlockSpec((g, share, INNER, INNER), lambda i, w: (0, 0, 0, 0)) for g in groups],
        ),
        out_shape=[jax.ShapeDtypeStruct((g, share, INNER, INNER), f32) for g in groups],
        compiler_params=params(),
        cost_estimate=pl.CostEstimate(flops=1 << 20, bytes_accessed=2 << 20, transcendentals=0),
    )(jnp.stack([local, first, pencil]), *[kernel_spectra] * share)
    mirrored = lax.ppermute(moved[0], "pencil", [(p, (pencils - p) % pencils) for p in range(pencils)])
    if per > 1:
        rest = lax.ppermute(moved[1], "pencil", [(p, pencils - 1 - p) for p in range(pencils)])

    offset = lax.dynamic_index_in_dim(background[:, 0], member_ids[0], 0, keepdims=True)
    row_high, row_low = halves(row_tables())
    block = min(part_rows, 128)
    sent = pl.pallas_call(
        functools.partial(rows_kernel, pencils, width),
        grid=(part_rows // block,),
        in_specs=[
            smem,
            pl.BlockSpec((None, None, block, LENGTH), lambda i: (0, 0, i, 0)),
            pl.BlockSpec((8, 512, 256), lambda i: (0, 0, 0)),
            pl.BlockSpec((8, 512, 256), lambda i: (0, 0, 0)),
        ],
        out_specs=[pl.BlockSpec((pencils, 2, block, lanes), lambda i: (0, 0, i, 0))] * chunks,
        out_shape=[jax.ShapeDtypeStruct((pencils, 2, part_rows, lanes), f32)] * chunks,
        scratch_shapes=[pltpu.VMEM((8, block, 256), f32)],
        compiler_params=params(),
        cost_estimate=pl.CostEstimate(flops=6 * part_rows * 2 * LENGTH * 512, bytes_accessed=12 << 20, transcendentals=0),
    )(offset, density, row_high, row_low)
    arrived = [lax.all_to_all(part, "pencil", 0, 0, tiled=True) for part in sent]

    sign = jnp.array([0.5, -0.5], f32)
    edge = lax.dynamic_slice(kernel_spectra, (local, 0, 0, HALF), (1, 2, LENGTH, 1))
    edge = edge.reshape(2, RADIX, INNER).astype(f32)
    flipped = jnp.concatenate([edge[:, :1], edge[:, :0:-1]], axis=1)[..., ::-1]
    flipped = jnp.concatenate([jnp.roll(flipped[:, :1], 1, axis=2), flipped[:, 1:]], axis=1)
    edge = 0.5 * edge + sign.reshape(2, 1, 1) * flipped
    edge = jnp.where(lax.broadcasted_iota(jnp.int32, (lanes,), 0) == 0, edge[..., None], 0.0)

    if per > 1:
        mirrored = jnp.concatenate([mirrored, rest], axis=0)
    mirrored, edge, _ = lax.optimization_barrier((mirrored, edge, sent[0]))
    mirrored = lax.all_gather(mirrored, ("grp", "mem"), axis=0)

    column, column_turns = column_tables()
    column_turns = jnp.asarray(column_turns)
    tables = jnp.stack(halves(column) + halves(column.T))
    two = depths == 2
    mine = lax.axis_index("depth") if two else jnp.int32(0)
    where = jnp.stack([mine, local, pencil])
    fields = []
    before = None
    for k in range(chunks):
        special = k == 0
        steps = sharers

        def early(i, special=special):
            return jnp.minimum(i, steps - 1) if special else i

        def late(i, special=special):
            return jnp.maximum(i - steps, 0) if special else i

        here = arrived[k]
        if before is not None:
            here, before = lax.optimization_barrier((here, before))
            fields.append(lax.all_to_all(before, "pencil", 0, 0, tiled=True))
        edge_block = (2, share, INNER, lanes) if special else (2, 1, 8, lanes)
        out = pl.pallas_call(
            functools.partial(columns_kernel, special),
            grid_spec=pltpu.PrefetchScalarGridSpec(
                num_scalar_prefetch=1,
                grid=(2 * steps if special else steps,),
                in_specs=[
                    pl.BlockSpec((pencils, 2, part_rows, lanes), lambda i, w: (0, 0, 0, 0)),
                    pl.BlockSpec(
                        (None, 2, share * INNER, width * INNER), lambda i, w, k=k, late=late: (w[1], 0, late(i), k)
                    ),
                    pl.BlockSpec(
                        (None, width, share, INNER, INNER), lambda i, w, k=k, late=late: (late(i), k, 0, 0, 0)
                    ),
                    pl.BlockSpec(
                        edge_block,
                        (lambda i, w, late=late: (0, late(i), 0, 0)) if special else (lambda i, w: (0, 0, 0, 0)),
                    ),
                ]
                + [pl.BlockSpec((share, INNER, INNER), lambda i, w, early=early: (early(i), 0, 0))]
                + [pl.BlockSpec((share, INNER, INNER), lambda i, w, late=late: (late(i), 0, 0))]
                + [pl.BlockSpec((4, 256, 256), lambda i, w: (0, 0, 0))],
                out_specs=pl.BlockSpec((depths, pencils, 2, out_rows, lanes), lambda i, w: (0, 0, 0, 0, 0)),
                scratch_shapes=[
                    pltpu.VMEM((RADIX, 256, lanes), f32),
                    pltpu.VMEM((RADIX if special else 1, 256, lanes), f32),
                ],
            ),
            out_shape=jax.ShapeDtypeStruct((depths, pencils, 2, out_rows, lanes), f32),
            compiler_params=params(),
            cost_estimate=pl.CostEstimate(
                flops=12 * RADIX * 256 * 256 * lanes, bytes_accessed=16 << 20, transcendentals=0
            ),
        )(where, here, kernel_spectra, mirrored, edge, column_turns, column_turns, tables)
        if two:
            before = out[0] + lax.ppermute(out[1], "depth", [(0, 1), (1, 0)])
        else:
            before = lax.psum_scatter(out, "depth", scatter_dimension=0, tiled=False)
    fields.append(lax.all_to_all(before, "pencil", 0, 0, tiled=True))

    back_high, back_low = halves(inverse_row_tables())
    return pl.pallas_call(
        functools.partial(fields_kernel, pencils, width, [1] * chunks),
        in_specs=[vmem] * (len(fields) + 2),
        out_specs=vmem,
        out_shape=jax.ShapeDtypeStruct((1, out_rows, LENGTH), f32),
        scratch_shapes=[pltpu.VMEM((8, out_rows, 256), f32)],
        compiler_params=params(),
        cost_estimate=pl.CostEstimate(flops=6 * out_rows * 2 * LENGTH * 512, bytes_accessed=8 << 20, transcendentals=0),
    )(*fields, back_high, back_low)


def solution(mesh):
    placed = (
        P(("grp", "mem"), "depth", "pencil", None),
        P(None, "depth"),
        P(("grp", "mem")),
        P("depth"),
        P("depth", None, None, "pencil"),
    )
    return jax.shard_map(
        body,
        mesh=mesh,
        in_specs=placed,
        out_specs=P(("grp", "mem"), ("pencil", "depth"), None),
        check_vma=False,
    )
```

```python
import functools
import math

import jax
import jax.numpy as jnp
import numpy as np
from jax import lax
from jax.experimental import pallas as pl
from jax.experimental.pallas import tpu as pltpu
from jax.sharding import PartitionSpec as P

RADIX = 16
INNER = 128
HALF = 64
LENGTH = RADIX * INNER
f32 = jnp.float32
bf16 = jnp.bfloat16


def halves(table):
    table = np.asarray(table, np.float32)
    high = table.astype(bf16)
    low = (table - high.astype(np.float32)).astype(bf16)
    return jnp.asarray(high), jnp.asarray(low)


def residue_rows(r):
    m = np.arange(INNER)[:, None]
    q = np.arange(HALF)[None, :]
    turn = np.exp(-2j * np.pi * (((RADIX * q + r) * m) % LENGTH) / LENGTH)
    re, im = turn.real.copy(), turn.imag.copy()
    if r == 0:
        im[:, 0] = (-1.0) ** m[:, 0]
    out = np.zeros((2 * INNER, 2 * HALF))
    if r == 0:
        out[:INNER, :HALF], out[:INNER, HALF:] = re, im
    elif r == 8:
        out[INNER:, :HALF], out[INNER:, HALF:] = re, im
    else:
        sign = 1.0 if r < 8 else -1.0
        out[:INNER, :HALF], out[:INNER, HALF:] = re, im
        out[INNER:, :HALF], out[INNER:, HALF:] = -sign * im, sign * re
    return out


def slot_of(r):
    return 0 if r in (0, 8) else min(r, RADIX - r)


def row_tables():
    tables = np.zeros((8, 512, 256))
    for t in range(8):
        for odd in range(2):
            block = residue_rows(2 * t + odd)
            rows = slice(256 * odd, 256 * odd + 256)
            tables[t, rows, HALF * odd : HALF * odd + HALF] = block[:, :HALF]
            tables[t, rows, 128 + HALF * odd : 128 + HALF * odd + HALF] = block[:, HALF:]
    return tables


def inverse_row_tables():
    tables = np.zeros((8, 512, 256))
    scale = 1.0 / (LENGTH * LENGTH)
    for s in range(8):
        for place, r in enumerate((s, 8 if s == 0 else RADIX - s)):
            block = residue_rows(r).T.copy() * scale
            weight = np.full((2 * HALF, 1), 2.0 if r in (0, 8) else 1.0)
            if r == 0:
                weight[0] = weight[HALF] = 1.0
            block *= weight
            odd = r % 2
            tables[s, 256 * place + HALF * odd : 256 * place + HALF * odd + HALF] += block[:HALF]
            tables[s, 256 * place + 128 + HALF * odd : 256 * place + 128 + HALF * odd + HALF] += block[HALF:]
    return tables


def column_tables():
    q = np.arange(INNER)[:, None]
    m = np.arange(INNER)[None, :]
    turn = np.exp(-2j * np.pi * ((q * m) % INNER) / INNER)
    table = np.block([[turn.real, -turn.imag], [turn.imag, turn.real]])
    angles = 2 * np.pi * np.arange(RADIX)[:, None] * np.arange(INNER)[None, :] / LENGTH
    turns = np.zeros((RADIX, INNER, INNER), np.float32)
    turns[..., 0] = np.cos(angles)
    turns[..., 1] = np.sin(angles)
    return table, turns


def split_value(value):
    high = value.astype(bf16)
    return high, (value - high.astype(f32)).astype(bf16)


def dot(a, b):
    return jnp.dot(a, b, preferred_element_type=f32)


def rotate(value, count, length, sign):
    re, im = value
    count %= length
    if count == 0:
        return value
    if 4 * count == length:
        return (im, -re) if sign < 0 else (-im, re)
    c = math.cos(2 * math.pi * count / length)
    s = sign * math.sin(2 * math.pi * count / length)
    if 8 * count == length:
        return ((re + im) * c, (im - re) * c) if sign < 0 else ((re - im) * c, (im + re) * c)
    return (re * c - im * s, re * s + im * c)


def plus(a, b):
    return (a[0] + b[0], a[1] + b[1])


def minus(a, b):
    return (a[0] - b[0], a[1] - b[1])


def transform(values, sign):
    length = len(values)
    if length == 1:
        return values
    even, odd = transform(values[0::2], sign), transform(values[1::2], sign)
    turned = [rotate(odd[k], k, length, sign) for k in range(length // 2)]
    return [plus(even[k], turned[k]) for k in range(length // 2)] + [
        minus(even[k], turned[k]) for k in range(length // 2)
    ]


def real_transform(values):
    length = len(values)
    if length == 2:
        return [(values[0] + values[1], None), (values[0] - values[1], None)]
    even, odd = real_transform(values[0::2]), real_transform(values[1::2])
    out = [None] * (length // 2 + 1)
    out[0] = (even[0][0] + odd[0][0], None)
    out[length // 2] = (even[0][0] - odd[0][0], None)
    quarter = length // 4
    for k in range(1, quarter):
        turned = rotate(odd[k], k, length, -1)
        out[k] = plus(even[k], turned)
        low = minus(even[k], turned)
        out[length // 2 - k] = (low[0], -low[1])
    out[quarter] = (even[quarter][0], -odd[quarter][0])
    return out


def real_inverse(values):
    half = len(values) - 1
    length = 2 * half
    if length == 2:
        return [values[0][0] + values[1][0], values[0][0] - values[1][0]]
    even, odd = [], []
    for k in range(half // 2 + 1):
        if k == 0:
            even.append((values[0][0] + values[half][0], None))
            odd.append((values[0][0] - values[half][0], None))
        elif k == half // 2:
            even.append((2.0 * values[k][0], None))
            odd.append((-2.0 * values[k][1], None))
        else:
            other = values[half - k]
            even.append((values[k][0] + other[0], values[k][1] - other[1]))
            odd.append(rotate((values[k][0] - other[0], values[k][1] + other[1]), k, length, 1))
    first, second = real_inverse(even), real_inverse(odd)
    return [x for pair in zip(first, second) for x in pair]


def rows_kernel(pencils, width, offset_ref, in_ref, high_ref, low_ref, *rest):
    outs, pieces = rest[:-1], rest[-1]
    rows = in_ref.shape[0]
    per = RADIX // pencils
    offset = offset_ref[0]

    def step(b, carry):
        at = pl.ds(pl.multiple_of(b * 8, 8), 8)
        values = [in_ref[at, n * INNER : (n + 1) * INNER] - offset for n in range(RADIX)]
        got = real_transform(values)
        pieces[0, at, :INNER] = got[0][0]
        pieces[0, at, INNER:] = got[8][0]
        for s in range(1, 8):
            pieces[s, at, :INNER] = got[s][0]
            pieces[s, at, INNER:] = got[s][1]
        return carry

    lax.fori_loop(0, rows // 8, step, 0)
    for t in range(8):
        total = None
        for odd in range(2):
            high, low = split_value(pieces[slot_of(2 * t + odd)])
            table_high = high_ref[t, 256 * odd : 256 * odd + 256]
            table_low = low_ref[t, 256 * odd : 256 * odd + 256]
            part = dot(high, table_high) + dot(low, table_high) + dot(high, table_low)
            total = part if total is None else total + part
        if width == 2:
            pencil, place = divmod(2 * t, per)
            for c in range(2):
                outs[place // 2][pencil, c] = total[:, c * 128 : (c + 1) * 128]
        else:
            for odd in range(2):
                pencil, place = divmod(2 * t + odd, per)
                for c in range(2):
                    begin = c * 128 + odd * HALF
                    outs[place][pencil, c] = total[:, begin : begin + HALF]


def swapped(zero, shape, axis):
    total = lax.broadcasted_iota(jnp.int32, shape, 0) + lax.broadcasted_iota(jnp.int32, shape, 1)
    wanted = jnp.where(zero, INNER, INNER - 1)
    also = jnp.where(zero, 0, INNER - 1)
    return jnp.where((total == wanted) | (total == also), 1.0, 0.0).astype(bf16)


def mirror_kernel(share, where_ref, *refs):
    ins, zero_ref, rest_refs = refs[:share], refs[share], refs[share + 1 :]
    per = ins[0].shape[2] // INNER
    plain = swapped(where_ref[1] < 0, (INNER, HALF), 1)
    edge = swapped(where_ref[2] == 0, (INNER, HALF), 1)
    for u in range(share):
        swap = swapped(where_ref[1] + u == 0, (INNER, INNER), 0)
        rows = [dot(swap, ins[u][c]).astype(bf16) for c in range(2)]
        for j in range(per):
            turn = edge if j == 0 else plain
            turned = [dot(rows[c][:, j * INNER : (j + 1) * INNER], turn) for c in range(2)]
            value = jnp.concatenate(turned, axis=1)
            if j == 0:
                zero_ref[0, u] = value
            else:
                rest_refs[0][per - 1 - j, u] = value


def columns_kernel(special, where_ref, in_ref, kern_ref, mirror_ref, edge_ref,
                   turns_ref, late_ref, table_ref, out_ref, pieces, waves):
    part_rows = in_ref.shape[2]
    depths, pencils, _, out_rows, lanes = out_ref.shape
    share = mirror_ref.shape[1]
    steps = RADIX // share
    mine = where_ref[0]
    now = pl.program_id(0)
    from_lane = lax.broadcasted_iota(jnp.int32, (kern_ref.shape[2], lanes), 0)
    to_lane = lax.broadcasted_iota(jnp.int32, (kern_ref.shape[2], lanes), 1)
    wanted = to_lane + jnp.where(to_lane < HALF, 0, HALF)
    pick = jnp.where(from_lane == wanted, 0.5, 0.0).astype(bf16)
    zero_swap = swapped(mine >= 0, (INNER, INNER), 0)
    plain_swap = swapped(mine < 0, (INNER, INNER), 0)

    def forward(b, carry):
        values = []
        for n in range(RADIX):
            source, begin = divmod(n * INNER, part_rows)
            at = pl.ds(pl.multiple_of(begin + b * 8, 8), 8)
            values.append((in_ref[source, 0, at, :], in_ref[source, 1, at, :]))
        at = pl.ds(pl.multiple_of(b * 8, 8), 8)
        also = pl.ds(pl.multiple_of(INNER + b * 8, 8), 8)
        for r, (re, im) in enumerate(transform(values, -1)):
            pieces[r, at, :] = re
            pieces[r, also, :] = im
        return carry

    @pl.when(now == 0)
    def _():
        lax.fori_loop(0, INNER // 8, forward, 0)

    def wave(r, u):
        re, im = pieces[r, :INNER], pieces[r, INNER:]
        c, s = turns_ref[u, :, 0:1], turns_ref[u, :, 1:2]
        high, low = split_value(jnp.concatenate([re * c + im * s, im * c - re * s], axis=0))
        return dot(table_ref[0], high) + dot(table_ref[0], low) + dot(table_ref[1], high)

    def finish(r, u, got):
        re, im = got[:INNER], got[INNER:]
        tiles = [mirror_ref[j, u] for j in range(mirror_ref.shape[0])]
        rows = slice(u * INNER, (u + 1) * INNER)
        parts = []
        for c in range(2):
            other = [tile[:, c * HALF : (c + 1) * HALF] for tile in tiles]
            other = jnp.concatenate(other, axis=1) if len(other) > 1 else other[0]
            own = dot(kern_ref[c, rows, :], pick)
            parts.append(own + 0.5 * other if c == 0 else own - 0.5 * other)
        kr, ki = parts
        if special:
            other = lax.rem(RADIX - r, RADIX)
            high, low = split_value(waves[other])
            swap = jnp.where(r == 0, zero_swap.astype(f32), plain_swap.astype(f32)).astype(bf16) if u == 0 else plain_swap
            ore = dot(swap, high[:INNER]) + dot(swap, low[:INNER])
            oim = -(dot(swap, high[INNER:]) + dot(swap, low[INNER:]))
            mask = (lax.broadcasted_iota(jnp.int32, (INNER, lanes), 1) == 0) & (where_ref[2] == 0)
            hr = jnp.where(mask, 0.5 * (kr - edge_ref[0, u]), 0.0)
            hi = jnp.where(mask, 0.5 * (ki - edge_ref[1, u]), 0.0)
            kr, ki = kr - hr, ki - hi
            sr = re * kr - im * ki + (ore * hr - oim * hi)
            si = re * ki + im * kr + (ore * hi + oim * hr)
        else:
            sr, si = re * kr - im * ki, re * ki + im * kr
        spectrum = jnp.concatenate([sr, si], axis=0)
        high, low = split_value(spectrum)
        got = dot(table_ref[2], high) + dot(table_ref[2], low) + dot(table_ref[3], high)
        re, im = got[:INNER], got[INNER:]
        c, s = late_ref[u, :, 0:1], late_ref[u, :, 1:2]
        pieces[r, :INNER] = re * c - im * s
        pieces[r, INNER:] = im * c + re * s

    if special:
        @pl.when(now < steps)
        def _():
            for u in range(share):
                waves[now * share + u] = wave(now * share + u, u)

        @pl.when(now >= steps)
        def _():
            for u in range(share):
                r = (now - steps) * share + u
                finish(r, u, waves[r])
    else:
        for u in range(share):
            r = now * share + u
            finish(r, u, wave(r, u))

    slots = [lax.rem(d - mine + depths, depths) for d in range(depths)]

    def backward(b, carry):
        at = pl.ds(pl.multiple_of(b * 8, 8), 8)
        also = pl.ds(pl.multiple_of(INNER + b * 8, 8), 8)
        values = [(pieces[r, at, :], pieces[r, also, :]) for r in range(RADIX)]
        for n, (re, im) in enumerate(transform(values, 1)):
            if out_rows % INNER == 0:
                part, begin = divmod(n * INNER, out_rows)
                pencil, depth = divmod(part, depths)
                depth = slots[depth]
                put = pl.ds(pl.multiple_of(begin + b * 8, 8), 8)
            else:
                x = n * INNER + b * 8
                pencil = x // (out_rows * depths)
                depth = lax.rem(x // out_rows - mine + depths, depths)
                put = pl.ds(pl.multiple_of(lax.rem(x, out_rows), 8), 8)
            out_ref[depth, pencil, 0, put, :] = re
            out_ref[depth, pencil, 1, put, :] = im
        return carry

    @pl.when(now == pl.num_programs(0) - 1)
    def _():
        lax.fori_loop(0, INNER // 8, backward, 0)


def fields_kernel(pencils, width, counts, *refs):
    ins, at = [], 0
    for count in counts:
        ins.append(refs[at : at + count])
        at += count
    high_ref, low_ref, out_ref, pieces = refs[at:]
    per = RADIX // pencils
    rows = out_ref.shape[1]

    def read(chunk, pencil, c):
        found = [ref[pencil, c] for ref in ins[chunk]]
        return jnp.concatenate(found, axis=0) if len(found) > 1 else found[0]

    def pair(t):
        if width == 2:
            pencil, place = divmod(2 * t, per)
            return jnp.concatenate([read(place // 2, pencil, c) for c in range(2)], axis=1)
        found = []
        for c in range(2):
            for odd in range(2):
                pencil, place = divmod(2 * t + odd, per)
                found.append(read(place, pencil, c))
        return jnp.concatenate(found, axis=1)

    for s in range(8):
        total = None
        for place, r in enumerate((s, 8 if s == 0 else RADIX - s)):
            high, low = split_value(pair(r // 2))
            table_high = high_ref[s, 256 * place : 256 * place + 256]
            table_low = low_ref[s, 256 * place : 256 * place + 256]
            part = dot(high, table_high) + dot(low, table_high) + dot(high, table_low)
            total = part if total is None else total + part
        pieces[s] = total

    def step(b, carry):
        at = pl.ds(pl.multiple_of(b * 8, 8), 8)
        values = [(pieces[0, at, :INNER], None)]
        for s in range(1, 8):
            values.append((pieces[s, at, :INNER], pieces[s, at, INNER:]))
        values.append((pieces[0, at, INNER:], None))
        for n, value in enumerate(real_inverse(values)):
            out_ref[0, at, n * INNER : (n + 1) * INNER] = value
        return carry

    lax.fori_loop(0, rows // 8, step, 0)


def params(**more):
    return pltpu.CompilerParams(vmem_limit_bytes=48 * 1024 * 1024, **more)


def body(density, background, member_ids, layer_kernel, kernel_spectra):
    pencils = lax.axis_size("pencil")
    depths = lax.axis_size("depth")
    sharers = lax.axis_size("grp") * lax.axis_size("mem")
    pencil = lax.axis_index("pencil")
    per = RADIX // pencils
    width = min(per, 2)
    chunks = per // width
    lanes = width * HALF
    part_rows = density.shape[2]
    out_rows = part_rows // depths
    vmem = pl.BlockSpec(memory_space=pltpu.VMEM)
    smem = pl.BlockSpec(memory_space=pltpu.SMEM)

    kern_count = kernel_spectra.shape[0]
    local = layer_kernel[0] - lax.axis_index("depth") * kern_count
    share = RADIX // sharers
    first = lax.axis_index(("grp", "mem")) * share
    groups = [1] if per == 1 else [1, per - 1]
    moved = pl.pallas_call(
        functools.partial(mirror_kernel, share),
        grid_spec=pltpu.PrefetchScalarGridSpec(
            num_scalar_prefetch=1,
            grid=(1,),
            in_specs=[
                pl.BlockSpec(
                    (None, 2, INNER, per * INNER),
                    lambda i, w, u=u: (w[0], 0, lax.rem(RADIX - w[1] - u, RADIX), 0),
                )
                for u in range(share)
            ],
            out_specs=[pl.BlockSpec((g, share, INNER, INNER), lambda i, w: (0, 0, 0, 0)) for g in groups],
        ),
        out_shape=[jax.ShapeDtypeStruct((g, share, INNER, INNER), f32) for g in groups],
        compiler_params=params(),
        cost_estimate=pl.CostEstimate(flops=1 << 20, bytes_accessed=2 << 20, transcendentals=0),
    )(jnp.stack([local, first, pencil]), *[kernel_spectra] * share)
    mirrored = lax.ppermute(moved[0], "pencil", [(p, (pencils - p) % pencils) for p in range(pencils)])
    if per > 1:
        rest = lax.ppermute(moved[1], "pencil", [(p, pencils - 1 - p) for p in range(pencils)])

    offset = lax.dynamic_index_in_dim(background[:, 0], member_ids[0], 0, keepdims=True)
    row_high, row_low = halves(row_tables())
    block = min(part_rows, 128)
    sent = pl.pallas_call(
        functools.partial(rows_kernel, pencils, width),
        grid=(part_rows // block,),
        in_specs=[
            smem,
            pl.BlockSpec((None, None, block, LENGTH), lambda i: (0, 0, i, 0)),
            pl.BlockSpec((8, 512, 256), lambda i: (0, 0, 0)),
            pl.BlockSpec((8, 512, 256), lambda i: (0, 0, 0)),
        ],
        out_specs=[pl.BlockSpec((pencils, 2, block, lanes), lambda i: (0, 0, i, 0))] * chunks,
        out_shape=[jax.ShapeDtypeStruct((pencils, 2, part_rows, lanes), f32)] * chunks,
        scratch_shapes=[pltpu.VMEM((8, block, 256), f32)],
        compiler_params=params(),
        cost_estimate=pl.CostEstimate(flops=6 * part_rows * 2 * LENGTH * 512, bytes_accessed=12 << 20, transcendentals=0),
    )(offset, density, row_high, row_low)
    arrived = [lax.all_to_all(part, "pencil", 0, 0, tiled=True) for part in sent]

    sign = jnp.array([0.5, -0.5], f32)
    edge = lax.dynamic_slice(kernel_spectra, (local, 0, 0, HALF), (1, 2, LENGTH, 1))
    edge = edge.reshape(2, RADIX, INNER).astype(f32)
    flipped = jnp.concatenate([edge[:, :1], edge[:, :0:-1]], axis=1)[..., ::-1]
    flipped = jnp.concatenate([jnp.roll(flipped[:, :1], 1, axis=2), flipped[:, 1:]], axis=1)
    edge = 0.5 * edge + sign.reshape(2, 1, 1) * flipped
    edge = jnp.where(lax.broadcasted_iota(jnp.int32, (lanes,), 0) == 0, edge[..., None], 0.0)

    if per > 1:
        mirrored = jnp.concatenate([mirrored, rest], axis=0)
    mirrored, edge, _ = lax.optimization_barrier((mirrored, edge, sent[0]))
    mirrored = lax.all_gather(mirrored, ("grp", "mem"), axis=0)

    column, column_turns = column_tables()
    column_turns = jnp.asarray(column_turns)
    tables = jnp.stack(halves(column) + halves(column.T))
    two = depths == 2
    mine = lax.axis_index("depth") if two else jnp.int32(0)
    where = jnp.stack([mine, local, pencil])
    fields = []
    before = None
    for k in range(chunks):
        special = k == 0
        steps = sharers

        def early(i, special=special):
            return jnp.minimum(i, steps - 1) if special else i

        def late(i, special=special):
            return jnp.maximum(i - steps, 0) if special else i

        here = arrived[k]
        if before is not None:
            here, before = lax.optimization_barrier((here, before))
            fields.append(lax.all_to_all(before, "pencil", 0, 0, tiled=True))
        edge_block = (2, share, INNER, lanes) if special else (2, 1, 8, lanes)
        out = pl.pallas_call(
            functools.partial(columns_kernel, special),
            grid_spec=pltpu.PrefetchScalarGridSpec(
                num_scalar_prefetch=1,
                grid=(2 * steps if special else steps,),
                in_specs=[
                    pl.BlockSpec((pencils, 2, part_rows, lanes), lambda i, w: (0, 0, 0, 0)),
                    pl.BlockSpec(
                        (None, 2, share * INNER, width * INNER), lambda i, w, k=k, late=late: (w[1], 0, late(i), k)
                    ),
                    pl.BlockSpec(
                        (None, width, share, INNER, INNER), lambda i, w, k=k, late=late: (late(i), k, 0, 0, 0)
                    ),
                    pl.BlockSpec(
                        edge_block,
                        (lambda i, w, late=late: (0, late(i), 0, 0)) if special else (lambda i, w: (0, 0, 0, 0)),
                    ),
                ]
                + [pl.BlockSpec((share, INNER, INNER), lambda i, w, early=early: (early(i), 0, 0))]
                + [pl.BlockSpec((share, INNER, INNER), lambda i, w, late=late: (late(i), 0, 0))]
                + [pl.BlockSpec((4, 256, 256), lambda i, w: (0, 0, 0))],
                out_specs=pl.BlockSpec((depths, pencils, 2, out_rows, lanes), lambda i, w: (0, 0, 0, 0, 0)),
                scratch_shapes=[
                    pltpu.VMEM((RADIX, 256, lanes), f32),
                    pltpu.VMEM((RADIX if special else 1, 256, lanes), f32),
                ],
            ),
            out_shape=jax.ShapeDtypeStruct((depths, pencils, 2, out_rows, lanes), f32),
            compiler_params=params(),
            cost_estimate=pl.CostEstimate(
                flops=12 * RADIX * 256 * 256 * lanes, bytes_accessed=16 << 20, transcendentals=0
            ),
        )(where, here, kernel_spectra, mirrored, edge, column_turns, column_turns, tables)
        if two:
            before = out[0] + lax.ppermute(out[1], "depth", [(0, 1), (1, 0)])
        else:
            before = lax.psum_scatter(out, "depth", scatter_dimension=0, tiled=False)
    fields.append(lax.all_to_all(before, "pencil", 0, 0, tiled=True))

    back_high, back_low = halves(inverse_row_tables())
    return pl.pallas_call(
        functools.partial(fields_kernel, pencils, width, [1] * chunks),
        in_specs=[vmem] * (len(fields) + 2),
        out_specs=vmem,
        out_shape=jax.ShapeDtypeStruct((1, out_rows, LENGTH), f32),
        scratch_shapes=[pltpu.VMEM((8, out_rows, 256), f32)],
        compiler_params=params(),
        cost_estimate=pl.CostEstimate(flops=6 * out_rows * 2 * LENGTH * 512, bytes_accessed=8 << 20, transcendentals=0),
    )(*fields, back_high, back_low)


def solution(mesh):
    placed = (
        P(("grp", "mem"), "depth", "pencil", None),
        P(None, "depth"),
        P(("grp", "mem")),
        P("depth"),
        P("depth", None, None, "pencil"),
    )
    return jax.shard_map(
        body,
        mesh=mesh,
        in_specs=placed,
        out_specs=P(("grp", "mem"), ("pencil", "depth"), None),
        check_vma=False,
    )
```
